32 devices in a mesh: ctx: 8 (over z, y), exp: 2 (over x), rep: 2 (over core).
Axes of the slice: x: 2, y: 2, z: 4, core: 2. Of those that a mesh axis runs over, the one named last changes fastest.
Arguments:
- queries: bfloat16 [1024, 4096], P(('rep', 'ctx'), 'exp'), parts along dimension 0, may hold values from -8 to 8
- key_rows: bfloat16 [1024, 256], P(('rep', 'ctx')), parts along dimension 0, may hold values from -8 to 8
- value_head_rows: bfloat16 [1024, 256], P(('rep', 'ctx')), parts along dimension 0, may hold values from -6 to 6
- block_order: int32 [16], P('rep'), parts along dimension 0, may hold values from 0 to 7, each once
- residual: bfloat16 [1024, 4096], P(('rep', 'ctx'), 'exp'), parts along dimension 0, may hold values from -8 to 8
- norm_gain: float32 [4096], P('exp'), may hold values from 0.25 to 1.75
- expert_ids: int32 [1024, 8], P(('rep', 'ctx')), parts along dimension 0, may hold values from 0 to 15, all different within a row; in each aligned block of 64 rows (0 to 63, 64 to 127, ...) at most 64 rows name the same one
- route_weight: float32 [1024, 8], P(('rep', 'ctx')), parts along dimension 0, may hold values from 0.02 to 0.5
- gate_weight: bfloat16 [16, 4096, 768], P('ctx', 'exp'), may hold values from -0.09375 to 0.09375
- up_weight: bfloat16 [16, 4096, 768], P('ctx', 'exp'), may hold values from -0.09375 to 0.09375
- down_weight: bfloat16 [16, 768, 4096], P('ctx', None, 'exp'), may hold values from -0.21875 to 0.21875
Outputs:
- layer_out: bfloat16 [1024, 4096], P(('rep', 'ctx'), 'exp'), parts along dimension 0
The draws below stay inside these ranges and needn't reach their ends.
There are 2 independent parts, one for each index of `rep`. The reference program is written for one: setup_inputs(seed, part) draws one part's arguments, and reference() takes and returns one part's arrays. A program takes and returns all parts, laid end to end along the dimension named above; an argument that names none is the same for every part. Nothing has to cross between parts.
Inputs may be any that keep to these rules, and one draw needn't show every extreme that they name: `expert_ids`: each row names 8 different experts. In each aligned block of 64 rows no expert is named by more than 64 rows, a bound that some block reaches. `block_order`: each block index appears once.
All inputs are finite; a program needn't handle non-finite values.
Results may differ from the reference program's by a relative error of at most 0.011.
Values may be sent and summed in bfloat16 or wider, within the bound.
No kernel may reach another device: no remote copies, remote signals or barrier semaphores. Data moves between devices by JAX's collectives and lax.ppermute only.
A program may use at most 64 MiB of HBM per device.

```python
import math
import jax
import jax.numpy as jnp
import numpy as np
from jax import lax

D = 4096
QUERY_HEADS = 32
KEY_VALUE_HEADS = 2
HEAD_SIZE = 128
HID = 768
TOPK = 8
TOKC = 64
PROMPT_LENGTH = 512
EXPERTS = 16
CAP = 64
N_CTX = 8
N_EXP = 2


def draw_queries(key, part):
    value_tensor = jnp.clip(jax.random.normal(jax.random.fold_in(key, 1), (PROMPT_LENGTH, QUERY_HEADS * HEAD_SIZE), jnp.float32), -6.0, 6.0)
    return value_tensor.astype(jnp.bfloat16)


def draw_key_rows(key, part):
    value_tensor = jnp.clip(jax.random.normal(jax.random.fold_in(key, 4), (PROMPT_LENGTH, KEY_VALUE_HEADS * HEAD_SIZE), jnp.float32), -6.0, 6.0)
    return value_tensor.astype(jnp.bfloat16)


def draw_residual(key, part):
    column = jnp.arange(D, dtype=jnp.float32)
    rising = 0.5 * jnp.exp(math.log(3.0) * column / D)
    jitter = jnp.exp(jax.random.uniform(jax.random.fold_in(key, 11), (1, D), jnp.float32, -0.4, 0.4))
    value_tensor = jax.random.normal(jax.random.fold_in(key, 12), (PROMPT_LENGTH, D), jnp.float32)
    return jnp.clip(value_tensor * rising[None, :] * jitter, -8.0, 8.0).astype(jnp.bfloat16)


def block_levels(rng, shape, shards, low, top_value):
    def one(dim, parts):
        heights = jax.random.uniform(jax.random.fold_in(jax.random.fold_in(rng, 6), dim), (parts,), jnp.float32, low / len(shards), top_value / len(shards))
        return jnp.repeat(jnp.exp(heights), shape[dim] // parts).reshape((-1,) + (1,) * (len(shape) - dim - 1))

    level = one(*shards[0])
    for cut in shards[1:]:
        level = level * one(*cut)
    return level


def shared_out(rng, own, number, rows, count, top, limit, slope):
    sequence = jax.random.permutation(rng, count)
    packed, usual = portions_of(count, rows * top, limit, slope, True), portions_of(count, rows * top, limit, slope, False)
    places = jnp.arange(count)

    def named(lengths, offset_by):
        used = int((lengths > 0).sum())
        fixed = max(1, used // 4)
        moved = fixed + (places - fixed + offset_by * (used - fixed)) % max(1, count - fixed)
        return jnp.zeros((count,), jnp.int32).at[sequence[jnp.where(places < fixed, places, moved)]].set(jnp.asarray(lengths, jnp.int32))

    lengths = jnp.where(number % 4 == 0, named(packed, number // 4), named(usual, number - number // 4 - 1))
    mixed = jax.random.permutation(jax.random.fold_in(own, 3), count)
    source_of, sink = mixed[0:count // 2 * 2:2], mixed[1:count // 2 * 2:2]
    room = jnp.minimum(lengths[source_of] - 1, limit - lengths[sink]) // 2
    room = jnp.where((source_of == sequence[0]) | (sink == sequence[0]) | (lengths[sink] == 0), 0, jnp.maximum(room, 0))
    moved = jax.random.randint(jax.random.fold_in(own, 4), (count // 2,), 0, 1 << 20) % (room + 1)
    lengths = lengths.at[source_of].add(-moved).at[sink].add(moved)
    members = jnp.searchsorted(jnp.cumsum(lengths), jnp.arange(rows * top), side="right").astype(jnp.int32)
    grid = members.reshape(top, rows).T
    grid = grid[jax.random.permutation(jax.random.fold_in(own, 1), rows)]
    offset_by = jax.random.randint(jax.random.fold_in(own, 2), (rows, 1), 0, top)
    return jnp.take_along_axis(grid, (jnp.arange(top)[None, :] + offset_by) % top, axis=1)


def portions_of(amount, total, bound, slope, full):
    weights = [(1 << 20) // math.isqrt(standing ** slope) + 1 for standing in range(1, amount + 1)]
    largest = bound if full else min(bound, max(-(-total // amount), total * weights[0] // sum(weights)))
    least = 1 if total - largest >= amount - 1 else 0
    holding, spare = [largest] + [least] * (amount - 1), total - largest - least * (amount - 1)
    while spare > 0:
        movable = [i for i in range(1, amount) if holding[i] < largest] or [i for i in range(1, amount) if holding[i] < bound]
        mass, remaining = sum([weights[i] for i in movable]), spare
        for i in movable:
            extra = min(bound - holding[i], max(1, remaining * weights[i] // mass), spare)
            holding[i] = holding[i] + extra
            spare = spare - extra
    return np.array(holding)


def scatter_about(key, extent, scale, limit, cuts=(), held_as=jnp.bfloat16):
    factor_of = block_levels(key, extent, cuts, -0.22, 0.18) if cuts else 1.0
    entries = jax.random.normal(key, extent, jnp.float32) * scale * factor_of
    return jnp.minimum(jnp.maximum(entries, -limit), limit).astype(held_as)


def setup_inputs(seed: int = 0, part: int = 0) -> dict:
    key_of = jax.random.split(jax.random.key(seed), 12)
    own_keys = jax.random.split(jax.random.fold_in(key_of[11], part), 12)
    queries = draw_queries(jax.random.fold_in(jax.random.fold_in(key_of[11], part), 71), part)
    key_rows = draw_key_rows(jax.random.fold_in(jax.random.fold_in(key_of[11], part), 71), part)
    value_head_rows = scatter_about(own_keys[2], (PROMPT_LENGTH, KEY_VALUE_HEADS * HEAD_SIZE), 1.0, 6.0, ((0, 8),))
    block_order = jax.random.permutation(own_keys[3], N_CTX).astype(jnp.int32)
    residual = draw_residual(jax.random.fold_in(jax.random.fold_in(key_of[11], part), 71), part)
    norm_gain = jnp.clip(1.0 + 0.15 * jax.random.normal(key_of[5], (D,), jnp.float32), 0.25, 1.75)
    expert_ids_keys = jax.random.split(jax.random.fold_in(own_keys[6], 1), PROMPT_LENGTH // TOKC)
    expert_ids_turns = jax.random.permutation(jax.random.fold_in(own_keys[6], 3), PROMPT_LENGTH // TOKC)
    expert_ids = jax.vmap(lambda own, number: shared_out(jax.random.fold_in(own_keys[6], 2), own, number, TOKC, EXPERTS, TOPK, CAP, 2))(expert_ids_keys, expert_ids_turns).reshape((PROMPT_LENGTH, TOPK))
    route_weight = jnp.clip(jnp.exp(math.log(0.5) - 3.218876 * jax.random.uniform(own_keys[7], (PROMPT_LENGTH, TOPK), jnp.float32) ** block_levels(own_keys[7], (PROMPT_LENGTH, TOPK), ((0, 8),), -0.2, 0.2)), 0.02, 0.5)
    gate_weight = scatter_about(key_of[8], (EXPERTS, D, HID), D ** -0.5, 0.09375, ((0, 8), (1, 2)))
    up_weight = scatter_about(key_of[9], (EXPERTS, D, HID), D ** -0.5, 0.09375, ((0, 8), (1, 2)))
    down_weight = scatter_about(key_of[10], (EXPERTS, HID, D), HID ** -0.5, 0.21875, ((0, 8), (2, 2)))
    return dict(queries=queries, key_rows=key_rows, value_head_rows=value_head_rows, block_order=block_order, residual=residual, norm_gain=norm_gain, expert_ids=expert_ids, route_weight=route_weight, gate_weight=gate_weight, up_weight=up_weight, down_weight=down_weight)


MASKED_SCORE = -1e+30
NORM_EPS = 1e-06

def reference(queries, key_rows, value_head_rows, block_order, residual, norm_gain, expert_ids, route_weight, gate_weight, up_weight, down_weight):
    row_index = jnp.arange(PROMPT_LENGTH, dtype=jnp.int32)
    positions = block_order[row_index // TOKC] * TOKC + row_index % TOKC
    query_group_size = QUERY_HEADS // KEY_VALUE_HEADS
    inv_scale = 1.0 / math.sqrt(HEAD_SIZE)
    visible = positions[None, :] <= positions[:, None]

    def one_head(head_id):
        query_head = lax.dynamic_slice_in_dim(queries, (head_id * HEAD_SIZE).astype(jnp.int32), HEAD_SIZE, 1)
        kv_start = (head_id // query_group_size * HEAD_SIZE).astype(jnp.int32)
        key_head = lax.dynamic_slice_in_dim(key_rows, kv_start, HEAD_SIZE, 1)
        value_head = lax.dynamic_slice_in_dim(value_head_rows, kv_start, HEAD_SIZE, 1)
        scores = jnp.dot(query_head, key_head.T, preferred_element_type=jnp.float32) * inv_scale
        scores = jnp.where(visible, scores, MASKED_SCORE)
        row_max = lax.optimization_barrier(jnp.max(scores, axis=1, keepdims=True))
        weights = jnp.where(visible, jnp.exp(scores - row_max), 0.0)
        weight_sum = lax.optimization_barrier(jnp.sum(weights, axis=1, keepdims=True))
        return jnp.dot(weights.astype(jnp.bfloat16), value_head, preferred_element_type=jnp.float32) / weight_sum
    per_head = lax.map(one_head, jnp.arange(QUERY_HEADS, dtype=jnp.int32))
    attention = jnp.transpose(per_head, (1, 0, 2)).reshape(PROMPT_LENGTH, QUERY_HEADS * HEAD_SIZE).astype(jnp.bfloat16)
    mixed_rows = (residual.astype(jnp.float32) + attention.astype(jnp.float32)).astype(jnp.bfloat16)
    mixed_f = mixed_rows.astype(jnp.float32)
    mean_square = lax.optimization_barrier(jnp.mean(mixed_f * mixed_f, axis=1, keepdims=True))
    normed = (mixed_f * lax.rsqrt(mean_square + NORM_EPS) * norm_gain.astype(jnp.float32)[None, :]).astype(jnp.bfloat16)
    flat_ids = expert_ids.reshape(N_CTX, TOKC * TOPK)
    onehot = (flat_ids[:, :, None] == jnp.arange(EXPERTS, dtype=jnp.int32)[None, None, :]).astype(jnp.int32)
    slot_rank = lax.optimization_barrier(jnp.sum((jnp.cumsum(onehot, axis=1) - onehot) * onehot, axis=2))
    shard_index = jnp.arange(N_CTX, dtype=jnp.int32)[:, None]
    slot_index = (flat_ids * (N_CTX * CAP) + shard_index * CAP + slot_rank).reshape(-1).astype(jnp.int32)
    token_index = (shard_index * TOKC + jnp.arange(TOKC * TOPK, dtype=jnp.int32)[None, :] // TOPK).reshape(-1).astype(jnp.int32)
    slot_total = EXPERTS * N_CTX * CAP
    slot_token = jnp.zeros((slot_total,), jnp.int32).at[slot_index].set(token_index).reshape(EXPERTS, N_CTX * CAP)
    slot_live = jnp.zeros((slot_total,), jnp.float32).at[slot_index].set(1.0).reshape(EXPERTS, N_CTX * CAP)
    slot_scale = jnp.zeros((slot_total,), jnp.float32).at[slot_index].set(route_weight.reshape(-1).astype(jnp.float32)).reshape(EXPERTS, N_CTX * CAP)
    feature_slice = D // N_EXP

    def expert_step(combined, expert):
        rows_of = slot_token[expert]
        inputs = jnp.where(slot_live[expert][:, None] > 0, normed[rows_of], jnp.zeros((), jnp.bfloat16))
        inputs = inputs.astype(jnp.float32).reshape(-1, N_EXP, feature_slice)
        gate_mat = gate_weight[expert].astype(jnp.float32).reshape(N_EXP, feature_slice, HID)
        up_mat = up_weight[expert].astype(jnp.float32).reshape(N_EXP, feature_slice, HID)
        gate_part = jnp.einsum('njd,jdh->jnh', inputs, gate_mat, precision=lax.Precision.HIGHEST)
        up_part = jnp.einsum('njd,jdh->jnh', inputs, up_mat, precision=lax.Precision.HIGHEST)
        gate_sum = lax.optimization_barrier(jnp.sum(lax.optimization_barrier(gate_part.astype(jnp.bfloat16)).astype(jnp.float32), axis=0))
        up_sum = lax.optimization_barrier(jnp.sum(lax.optimization_barrier(up_part.astype(jnp.bfloat16)).astype(jnp.float32), axis=0))
        hidden = (jax.nn.silu(gate_sum) * up_sum).astype(jnp.bfloat16)
        expert_out = jnp.dot(hidden, down_weight[expert], preferred_element_type=jnp.float32).astype(jnp.bfloat16)
        contrib = slot_scale[expert][:, None] * expert_out.astype(jnp.float32)
        return (combined.at[rows_of].add(contrib), None)
    routed_sum, _ = lax.scan(expert_step, jnp.zeros((PROMPT_LENGTH, D), jnp.float32), jnp.arange(EXPERTS, dtype=jnp.int32))
    return (mixed_f + routed_sum).astype(jnp.bfloat16)
```

```python
import math

import jax
import jax.numpy as jnp
from jax import lax
from jax.sharding import PartitionSpec as P

D = 4096
QUERY_HEADS = 32
KEY_VALUE_HEADS = 2
HEAD_SIZE = 128
TOPK = 8

MASKED_SCORE = -1e30
NORM_EPS = 1e-06


def xor_pairs(count, bit):
    return [(i, i ^ bit) for i in range(count)]


def bits_of(count):
    bits = []
    bit = count // 2
    while bit:
        bits.append(bit)
        bit //= 2
    return bits


def gather_rows(block, count):
    for bit in bits_of(count):
        block = jnp.concatenate([block, lax.ppermute(block, "ctx", xor_pairs(count, bit))], axis=0)
    return block


def offsets(count):
    found = [0]
    for bit in bits_of(count):
        found = found + [offset ^ bit for offset in found]
    return found


def scatter_sums(partial, count):
    for bit in reversed(bits_of(count)):
        half = partial.shape[0] // 2
        arrived = lax.ppermute(partial[half:].astype(jnp.bfloat16), "ctx", xor_pairs(count, bit))
        partial = partial[:half] + arrived.astype(jnp.float32)
    return partial


def local(
    queries,
    key_rows,
    value_head_rows,
    block_order,
    residual,
    norm_gain,
    expert_ids,
    route_weight,
    gate_weight,
    up_weight,
    down_weight,
):
    shard_rows = queries.shape[0]
    ctx_count = lax.axis_size("ctx")
    exp_count = lax.axis_size("exp")
    local_head = queries.shape[1] // HEAD_SIZE
    expert_index = lax.axis_index("exp")
    ctx_index = lax.axis_index("ctx")
    own_experts, _, hidden_size = gate_weight.shape
    expert_count = ctx_count * own_experts

    key_value_head = expert_index * local_head // (QUERY_HEADS // KEY_VALUE_HEADS)
    my_keys = lax.dynamic_slice_in_dim(key_rows, key_value_head * HEAD_SIZE, HEAD_SIZE, 1)
    my_values = lax.dynamic_slice_in_dim(value_head_rows, key_value_head * HEAD_SIZE, HEAD_SIZE, 1)
    experts = jnp.arange(expert_count, dtype=jnp.int32)
    route = jnp.sum(
        jnp.where(expert_ids[:, :, None] == experts[None, None, :], route_weight[:, :, None], 0.0),
        axis=1,
    )
    route_high = lax.reduce_precision(route, 8, 7)
    route_low = route - route_high
    packed = jnp.concatenate(
        [my_keys, my_values, route_high.astype(jnp.bfloat16), route_low.astype(jnp.bfloat16)], axis=1
    )
    gathered = gather_rows(packed, ctx_count)
    all_keys = gathered[:, :HEAD_SIZE]
    all_values = gathered[:, HEAD_SIZE : 2 * HEAD_SIZE]
    all_route = gathered[:, 2 * HEAD_SIZE :].astype(jnp.float32)
    all_route = all_route[:, :expert_count] + all_route[:, expert_count:]
    own_route = lax.dynamic_slice_in_dim(all_route, ctx_index * own_experts, own_experts, 1)

    owners = jnp.array(offsets(ctx_count), jnp.int32) ^ ctx_index
    block_ids = jnp.arange(ctx_count, dtype=jnp.int32)
    key_block = jnp.sum(
        jnp.where(owners[:, None] == block_ids[None, :], block_order[None, :], 0), axis=1
    )
    own_block = key_block[0]
    local_rows = jnp.arange(shard_rows, dtype=jnp.int32)
    query_pos = jnp.tile(own_block * shard_rows + local_rows, local_head)
    key_pos = (key_block[:, None] * shard_rows + local_rows[None, :]).reshape(-1)
    query_flat = (
        queries.reshape(shard_rows, local_head, HEAD_SIZE)
        .transpose(1, 0, 2)
        .reshape(local_head * shard_rows, HEAD_SIZE)
    )
    inv_scale = 1.0 / math.sqrt(HEAD_SIZE)
    visible = key_pos[None, :] <= query_pos[:, None]
    scores = (
        lax.dot_general(
            query_flat, all_keys, (((1,), (1,)), ((), ())), preferred_element_type=jnp.float32
        )
        * inv_scale
    )
    scores = jnp.where(visible, scores, MASKED_SCORE)
    newest = jnp.max(scores, axis=1)
    weights = jnp.where(visible, jnp.exp(scores - newest[:, None]), 0.0)
    weight_sum = jnp.sum(weights, axis=1)
    weighted = jnp.dot(weights.astype(jnp.bfloat16), all_values, preferred_element_type=jnp.float32)
    attention = (
        (weighted / weight_sum[:, None])
        .reshape(local_head, shard_rows, HEAD_SIZE)
        .transpose(1, 0, 2)
        .reshape(shard_rows, local_head * HEAD_SIZE)
        .astype(jnp.bfloat16)
    )
    mixed_rows = (residual.astype(jnp.float32) + attention.astype(jnp.float32)).astype(jnp.bfloat16)
    mixed_f = mixed_rows.astype(jnp.float32)
    square_sum = lax.psum(jnp.sum(mixed_f * mixed_f, axis=1), "exp")
    normed = (mixed_f * lax.rsqrt(square_sum[:, None] / D + NORM_EPS) * norm_gain[None, :]).astype(
        jnp.bfloat16
    )

    all_normed = gather_rows(normed, ctx_count)
    total = all_normed.shape[0]
    share = total // exp_count

    def partial_sums(rows):
        terms = []
        for k in range(own_experts):
            for weight in (gate_weight, up_weight):
                terms.append(jnp.dot(rows, weight[k], preferred_element_type=jnp.float32))
        return jnp.concatenate([term.astype(jnp.bfloat16) for term in terms], axis=1)

    if exp_count == 2:
        swap = [(0, 1), (1, 0)]
        others = lax.dynamic_slice_in_dim(all_normed, (1 - expert_index) * share, share, 0)
        mine = lax.dynamic_slice_in_dim(all_normed, expert_index * share, share, 0)
        arrived = lax.ppermute(partial_sums(others), "exp", swap)
        sums = partial_sums(mine).astype(jnp.float32) + arrived.astype(jnp.float32)
    else:
        sums = lax.psum_scatter(
            partial_sums(all_normed), "exp", scatter_dimension=0, tiled=True
        ).astype(jnp.float32)
    my_route = lax.dynamic_slice_in_dim(own_route, expert_index * share, share, 0)
    pieces = []
    for k in range(own_experts):
        gate_sum = sums[:, 2 * k * hidden_size : (2 * k + 1) * hidden_size]
        up_sum = sums[:, (2 * k + 1) * hidden_size : (2 * k + 2) * hidden_size]
        pieces.append((jax.nn.silu(gate_sum) * up_sum * my_route[:, k : k + 1]).astype(jnp.bfloat16))
    hidden = jnp.concatenate(pieces, axis=1)
    if exp_count == 2:
        other_hidden = lax.ppermute(hidden, "exp", swap)
        first = jnp.where(expert_index == 0, hidden, other_hidden)
        second = jnp.where(expert_index == 0, other_hidden, hidden)
        all_hidden = jnp.concatenate([first, second], axis=0)
    else:
        all_hidden = lax.all_gather(hidden, "exp", axis=0, tiled=True)
    down = down_weight.reshape(own_experts * hidden_size, down_weight.shape[2])
    partial = jnp.dot(all_hidden, down, preferred_element_type=jnp.float32)
    routed_sum = scatter_sums(partial, ctx_count)
    return (mixed_f + routed_sum).astype(jnp.bfloat16)


def solution(mesh):
    placed = (
        P(("rep", "ctx"), "exp"),
        P(("rep", "ctx"), None),
        P(("rep", "ctx"), None),
        P("rep"),
        P(("rep", "ctx"), "exp"),
        P("exp"),
        P(("rep", "ctx"), None),
        P(("rep", "ctx"), None),
        P("ctx", "exp", None),
        P("ctx", "exp", None),
        P("ctx", None, "exp"),
    )
    return jax.shard_map(
        local, mesh=mesh, in_specs=placed, out_specs=P(("rep", "ctx"), "exp"), check_vma=False
    )
```

```python
import functools
import math

import jax
import jax.numpy as jnp
from jax import lax
from jax.experimental import pallas as pl
from jax.experimental.pallas import tpu as pltpu
from jax.sharding import PartitionSpec as P

D = 4096
QUERY_HEADS = 32
KEY_VALUE_HEADS = 2
HEAD_SIZE = 128
TOPK = 8

MASKED_SCORE = -1e30
NORM_EPS = 1e-06
LANES = 128
KERNEL_BYTES = 16 * 1024 * 1024
CHUNKS = ((0, 4, 1), (2, 5, 6), (3, 7))


def xor_pairs(count, bit):
    return [(i, i ^ bit) for i in range(count)]


def bits_of(count):
    bits = []
    bit = count // 2
    while bit:
        bits.append(bit)
        bit //= 2
    return bits


def gather_rows(block, count):
    for bit in bits_of(count):
        block = jnp.concatenate([block, lax.ppermute(block, "ctx", xor_pairs(count, bit))], axis=0)
    return block


def offsets(count):
    found = [0]
    for bit in bits_of(count):
        found = found + [offset ^ bit for offset in found]
    return found


def scatter_sums(partial, count):
    for bit in reversed(bits_of(count)):
        half = partial.shape[0] // 2
        arrived = lax.ppermute(partial[half:].astype(jnp.bfloat16), "ctx", xor_pairs(count, bit))
        partial = partial[:half] + arrived.astype(jnp.float32)
    return partial


def routed_at_once(mixed_rows, norm_gain, own_route, gate_weight, up_weight, down_weight):
    ctx_count = lax.axis_size("ctx")
    own_experts, _, hidden_size = gate_weight.shape
    mixed_f = mixed_rows.astype(jnp.float32)
    square_sum = lax.psum(jnp.sum(mixed_f * mixed_f, axis=1), "exp")
    normed = (mixed_f * lax.rsqrt(square_sum[:, None] / D + NORM_EPS) * norm_gain[None, :]).astype(
        jnp.bfloat16
    )
    all_normed = gather_rows(normed, ctx_count)
    share = all_normed.shape[0] // lax.axis_size("exp")
    terms = []
    for k in range(own_experts):
        for weight in (gate_weight, up_weight):
            term = jnp.dot(all_normed, weight[k], preferred_element_type=jnp.float32)
            terms.append(term.astype(jnp.bfloat16))
    sums = lax.psum_scatter(
        jnp.concatenate(terms, axis=1), "exp", scatter_dimension=0, tiled=True
    ).astype(jnp.float32)
    my_route = lax.dynamic_slice_in_dim(own_route, lax.axis_index("exp") * share, share, 0)
    pieces = []
    for k in range(own_experts):
        gate_sum = sums[:, 2 * k * hidden_size : (2 * k + 1) * hidden_size]
        up_sum = sums[:, (2 * k + 1) * hidden_size : (2 * k + 2) * hidden_size]
        pieces.append((jax.nn.silu(gate_sum) * up_sum * my_route[:, k : k + 1]).astype(jnp.bfloat16))
    hidden = lax.all_gather(jnp.concatenate(pieces, axis=1), "exp", axis=0, tiled=True)
    down = down_weight.reshape(own_experts * hidden_size, down_weight.shape[2])
    partial = jnp.dot(hidden, down, preferred_element_type=jnp.float32)
    return scatter_sums(partial, ctx_count)


def prepared(blocks, gain_ref):
    rows = jnp.concatenate([block[...] for block in blocks], axis=0).astype(jnp.float32)
    squares = jnp.sum(rows * rows, axis=1, keepdims=True)
    return (rows * gain_ref[...]).astype(jnp.bfloat16), squares


def first_kernel(blocks, index_ref, gain_ref, gate_ref, up_ref, *rest):
    out_ref = rest[blocks]
    k = index_ref[0]
    size = gate_ref.shape[2]
    rows, squares = prepared(rest[:blocks], gain_ref)
    gate = jnp.dot(rows, gate_ref[k], preferred_element_type=jnp.float32)
    out_ref[:, :size] = gate.astype(jnp.bfloat16)
    up = jnp.dot(rows, up_ref[k], preferred_element_type=jnp.float32)
    out_ref[:, size : 2 * size] = up.astype(jnp.bfloat16)
    high = squares.astype(jnp.bfloat16)
    low = (squares - high.astype(jnp.float32)).astype(jnp.bfloat16)
    lane = lax.broadcasted_iota(jnp.int32, (rows.shape[0], LANES), 1)
    out_ref[:, 2 * size :] = jnp.where(
        lane == 0, high.astype(jnp.float32), low.astype(jnp.float32)
    ).astype(jnp.bfloat16)


def hidden_kernel(kept_ref, arrived_ref, route_ref, out_ref):
    size = out_ref.shape[1]
    tail = kept_ref[:, 2 * size :].astype(jnp.float32) + arrived_ref[:, 2 * size :].astype(
        jnp.float32
    )
    scale = lax.rsqrt((tail[:, :1] + tail[:, 1:2]) / D + NORM_EPS)
    gate = kept_ref[:, :size].astype(jnp.float32) + arrived_ref[:, :size].astype(jnp.float32)
    up = kept_ref[:, size : 2 * size].astype(jnp.float32) + arrived_ref[
        :, size : 2 * size
    ].astype(jnp.float32)
    gate = gate * scale
    up = up * (scale * route_ref[...])
    out_ref[...] = (gate / (1.0 + jnp.exp(-gate)) * up).astype(jnp.bfloat16)


def down_kernel(index_ref, hidden_ref, down_ref, out_ref):
    out_ref[...] = jnp.dot(
        hidden_ref[...], down_ref[index_ref[0]], preferred_element_type=jnp.float32
    )


def last_kernel(index_ref, hidden_ref, down_ref, before_ref, *outs):
    both = before_ref[...] + jnp.dot(
        hidden_ref[...], down_ref[index_ref[0]], preferred_element_type=jnp.float32
    )
    rows = outs[0].shape[0]
    for i, out_ref in enumerate(outs):
        out_ref[...] = both[i * rows : (i + 1) * rows].astype(out_ref.dtype)


def in_vmem(kernel, out_shape, *args, flops=0):
    specs = [
        pl.BlockSpec(memory_space=pltpu.SMEM if arg.dtype == jnp.int32 else pltpu.VMEM)
        for arg in args
    ]
    many = isinstance(out_shape, (list, tuple))
    out_spec = pl.BlockSpec(memory_space=pltpu.VMEM)
    return pl.pallas_call(
        kernel,
        out_shape=out_shape,
        in_specs=specs,
        out_specs=[out_spec] * len(out_shape) if many else out_spec,
        compiler_params=pltpu.CompilerParams(vmem_limit_bytes=KERNEL_BYTES),
        cost_estimate=pl.CostEstimate(flops=flops, bytes_accessed=0, transcendentals=0),
    )(*args)


def routed_in_chunks(mixed_rows, norm_gain, own_route, gate_weight, up_weight, down_weight):
    rows, features = mixed_rows.shape
    ctx_count = lax.axis_size("ctx")
    size = gate_weight.shape[2]
    mine = lax.axis_index("exp").astype(jnp.int32).reshape(1)
    other = 1 - mine
    swap = [(0, 1), (1, 0)]
    gain = norm_gain.reshape(1, features)
    route_mine = lax.dynamic_index_in_dim(own_route, mine[0], 1, keepdims=True)
    place = {offset: i for i, offset in enumerate(offsets(ctx_count))}

    def hop(block, offset):
        return lax.ppermute(block, "ctx", xor_pairs(ctx_count, offset))

    block = {0: mixed_rows}
    block[4], block[1], block[2] = hop(block[0], 4), hop(block[0], 1), hop(block[0], 2)
    block[6], block[5] = hop(block[4], 2), hop(block[4], 1)
    block[3] = hop(block[2], 1)
    block[7] = hop(block[6], 1)

    total = 0.0
    for chunk in CHUNKS:
        blocks = [block[offset] for offset in chunk]
        count = len(chunk) * rows
        first = functools.partial(first_kernel, len(chunk))
        shape = jax.ShapeDtypeStruct((count, 2 * size + LANES), jnp.bfloat16)
        cost = 4 * count * features * size
        weights = (gain, gate_weight, up_weight)
        sent = in_vmem(first, shape, other, *weights, *blocks, flops=cost)
        arrived = lax.ppermute(sent, "exp", swap)
        kept = in_vmem(first, shape, mine, *weights, *blocks, flops=cost)
        route = jnp.concatenate(
            [route_mine[place[o] * rows : (place[o] + 1) * rows] for o in chunk], axis=0
        )
        hidden = in_vmem(
            hidden_kernel, jax.ShapeDtypeStruct((count, size), jnp.bfloat16), kept, arrived, route
        )
        other_hidden = lax.ppermute(hidden, "exp", swap)
        before = in_vmem(
            down_kernel,
            jax.ShapeDtypeStruct((count, features), jnp.float32),
            mine,
            hidden,
            down_weight,
            flops=cost // 2,
        )
        shapes = [
            jax.ShapeDtypeStruct((rows, features), jnp.bfloat16 if offset else jnp.float32)
            for offset in chunk
        ]
        terms = in_vmem(
            last_kernel, shapes, other, other_hidden, down_weight, before, flops=cost // 2
        )
        for offset, term in zip(chunk, terms):
            total = total + (hop(term, offset).astype(jnp.float32) if offset else term)
    return total


def local(
    queries,
    key_rows,
    value_head_rows,
    block_order,
    residual,
    norm_gain,
    expert_ids,
    route_weight,
    gate_weight,
    up_weight,
    down_weight,
):
    shard_rows = queries.shape[0]
    ctx_count = lax.axis_size("ctx")
    exp_count = lax.axis_size("exp")
    local_head = queries.shape[1] // HEAD_SIZE
    expert_index = lax.axis_index("exp")
    ctx_index = lax.axis_index("ctx")
    own_experts, _, hidden_size = gate_weight.shape
    expert_count = ctx_count * own_experts

    key_value_head = expert_index * local_head // (QUERY_HEADS // KEY_VALUE_HEADS)
    my_keys = lax.dynamic_slice_in_dim(key_rows, key_value_head * HEAD_SIZE, HEAD_SIZE, 1)
    my_values = lax.dynamic_slice_in_dim(value_head_rows, key_value_head * HEAD_SIZE, HEAD_SIZE, 1)
    experts = jnp.arange(expert_count, dtype=jnp.int32)
    route = jnp.sum(
        jnp.where(expert_ids[:, :, None] == experts[None, None, :], route_weight[:, :, None], 0.0),
        axis=1,
    )
    route_high = lax.reduce_precision(route, 8, 7)
    route_low = route - route_high
    packed = jnp.concatenate(
        [my_keys, my_values, route_high.astype(jnp.bfloat16), route_low.astype(jnp.bfloat16)], axis=1
    )
    gathered = gather_rows(packed, ctx_count)
    all_keys = gathered[:, :HEAD_SIZE]
    all_values = gathered[:, HEAD_SIZE : 2 * HEAD_SIZE]
    all_route = gathered[:, 2 * HEAD_SIZE :].astype(jnp.float32)
    all_route = all_route[:, :expert_count] + all_route[:, expert_count:]
    own_route = lax.dynamic_slice_in_dim(all_route, ctx_index * own_experts, own_experts, 1)

    owners = jnp.array(offsets(ctx_count), jnp.int32) ^ ctx_index
    block_ids = jnp.arange(ctx_count, dtype=jnp.int32)
    key_block = jnp.sum(
        jnp.where(owners[:, None] == block_ids[None, :], block_order[None, :], 0), axis=1
    )
    own_block = key_block[0]
    local_rows = jnp.arange(shard_rows, dtype=jnp.int32)
    query_pos = jnp.tile(own_block * shard_rows + local_rows, local_head)
    key_pos = (key_block[:, None] * shard_rows + local_rows[None, :]).reshape(-1)
    query_flat = (
        queries.reshape(shard_rows, local_head, HEAD_SIZE)
        .transpose(1, 0, 2)
        .reshape(local_head * shard_rows, HEAD_SIZE)
    )
    inv_scale = 1.0 / math.sqrt(HEAD_SIZE)
    visible = key_pos[None, :] <= query_pos[:, None]
    scores = (
        lax.dot_general(
            query_flat, all_keys, (((1,), (1,)), ((), ())), preferred_element_type=jnp.float32
        )
        * inv_scale
    )
    scores = jnp.where(visible, scores, MASKED_SCORE)
    newest = jnp.max(scores, axis=1)
    weights = jnp.where(visible, jnp.exp(scores - newest[:, None]), 0.0)
    weight_sum = jnp.sum(weights, axis=1)
    weighted = jnp.dot(weights.astype(jnp.bfloat16), all_values, preferred_element_type=jnp.float32)
    attention = (
        (weighted / weight_sum[:, None])
        .reshape(local_head, shard_rows, HEAD_SIZE)
        .transpose(1, 0, 2)
        .reshape(shard_rows, local_head * HEAD_SIZE)
        .astype(jnp.bfloat16)
    )
    mixed_rows = (residual.astype(jnp.float32) + attention.astype(jnp.float32)).astype(jnp.bfloat16)
    mixed_f = mixed_rows.astype(jnp.float32)
    if exp_count == 2 and own_experts == 2 and ctx_count == 8:
        routed_sum = routed_in_chunks(
            mixed_rows, norm_gain, own_route, gate_weight, up_weight, down_weight
        )
    else:
        routed_sum = routed_at_once(
            mixed_rows, norm_gain, own_route, gate_weight, up_weight, down_weight
        )
    return (mixed_f + routed_sum).astype(jnp.bfloat16)


def solution(mesh):
    placed = (
        P(("rep", "ctx"), "exp"),
        P(("rep", "ctx"), None),
        P(("rep", "ctx"), None),
        P("rep"),
        P(("rep", "ctx"), "exp"),
        P("exp"),
        P(("rep", "ctx"), None),
        P(("rep", "ctx"), None),
        P("ctx", "exp", None),
        P("ctx", "exp", None),
        P("ctx", None, "exp"),
    )
    return jax.shard_map(
        local, mesh=mesh, in_specs=placed, out_specs=P(("rep", "ctx"), "exp"), check_vma=False
    )
```

```python
import functools
import math

import jax
import jax.numpy as jnp
from jax import lax
from jax.experimental import pallas as pl
from jax.experimental.pallas import tpu as pltpu
from jax.sharding import PartitionSpec as P

D = 4096
QUERY_HEADS = 32
KEY_VALUE_HEADS = 2
HEAD_SIZE = 128
TOPK = 8

MASKED_SCORE = -1e30
NORM_EPS = 1e-06
LANES = 128
KERNEL_BYTES = 16 * 1024 * 1024
ROUTE_LANES = 16
HELD = False
COST = 2e9
PACK_COST = 5
ATT_COST = 5
HOPS = ((0, 1), (0, 4), (4, 2), (4, 1), (6, 1), (0, 2), (2, 1))
CHUNKS = ((1,), (6, 5), (7, 4), (2, 3), (0,))
SENDS = {1: 1, 2: 2, 3: 3, 4: 4, 5: 1, 6: 2, 7: 7}
STEPS = (
    ("send", 0), ("keep", 0), ("send", 1), ("hidden", 0), ("keep", 1), ("send", 2),
    ("both", 0), ("hidden", 1), ("keep", 2), ("hidden", 2), ("send", 3), ("both", 1), ("keep", 3),
    ("both", 2), ("hidden", 3), ("send", 4), ("keep", 4), ("both", 3), ("hidden", 4), ("own", 4), ("end", 4),
)
OWN = {"own": 1, "end": 4}


def xor_pairs(count, bit):
    return [(i, i ^ bit) for i in range(count)]


def bits_of(count):
    bits = []
    bit = count // 2
    while bit:
        bits.append(bit)
        bit //= 2
    return bits


def gather_rows(block, count):
    for bit in bits_of(count):
        block = jnp.concatenate([block, lax.ppermute(block, "ctx", xor_pairs(count, bit))], axis=0)
    return block


def offsets(count):
    found = [0]
    for bit in bits_of(count):
        found = found + [offset ^ bit for offset in found]
    return found


def scatter_sums(partial, count):
    for bit in reversed(bits_of(count)):
        half = partial.shape[0] // 2
        arrived = lax.ppermute(partial[half:].astype(jnp.bfloat16), "ctx", xor_pairs(count, bit))
        partial = partial[:half] + arrived.astype(jnp.float32)
    return partial


def routed_at_once(mixed_rows, norm_gain, own_route, gate_weight, up_weight, down_weight):
    ctx_count = lax.axis_size("ctx")
    own_experts, _, hidden_size = gate_weight.shape
    mixed_f = mixed_rows.astype(jnp.float32)
    square_sum = lax.psum(jnp.sum(mixed_f * mixed_f, axis=1), "exp")
    normed = (mixed_f * lax.rsqrt(square_sum[:, None] / D + NORM_EPS) * norm_gain[None, :]).astype(
        jnp.bfloat16
    )
    all_normed = gather_rows(normed, ctx_count)
    share = all_normed.shape[0] // lax.axis_size("exp")
    terms = []
    for k in range(own_experts):
        for weight in (gate_weight, up_weight):
            term = jnp.dot(all_normed, weight[k], preferred_element_type=jnp.float32)
            terms.append(term.astype(jnp.bfloat16))
    sums = lax.psum_scatter(
        jnp.concatenate(terms, axis=1), "exp", scatter_dimension=0, tiled=True
    ).astype(jnp.float32)
    my_route = lax.dynamic_slice_in_dim(own_route, lax.axis_index("exp") * share, share, 0)
    pieces = []
    for k in range(own_experts):
        gate_sum = sums[:, 2 * k * hidden_size : (2 * k + 1) * hidden_size]
        up_sum = sums[:, (2 * k + 1) * hidden_size : (2 * k + 2) * hidden_size]
        pieces.append((jax.nn.silu(gate_sum) * up_sum * my_route[:, k : k + 1]).astype(jnp.bfloat16))
    hidden = lax.all_gather(jnp.concatenate(pieces, axis=1), "exp", axis=0, tiled=True)
    down = down_weight.reshape(own_experts * hidden_size, down_weight.shape[2])
    partial = jnp.dot(hidden, down, preferred_element_type=jnp.float32)
    return scatter_sums(partial, ctx_count)


def general(
    queries,
    key_rows,
    value_head_rows,
    block_order,
    residual,
    norm_gain,
    expert_ids,
    route_weight,
    gate_weight,
    up_weight,
    down_weight,
):
    shard_rows = queries.shape[0]
    ctx_count = lax.axis_size("ctx")
    local_head = queries.shape[1] // HEAD_SIZE
    expert_index = lax.axis_index("exp")
    ctx_index = lax.axis_index("ctx")
    own_experts = gate_weight.shape[0]
    expert_count = ctx_count * own_experts

    key_value_head = expert_index * local_head // (QUERY_HEADS // KEY_VALUE_HEADS)
    my_keys = lax.dynamic_slice_in_dim(key_rows, key_value_head * HEAD_SIZE, HEAD_SIZE, 1)
    my_values = lax.dynamic_slice_in_dim(value_head_rows, key_value_head * HEAD_SIZE, HEAD_SIZE, 1)
    experts = jnp.arange(expert_count, dtype=jnp.int32)
    route = jnp.sum(
        jnp.where(expert_ids[:, :, None] == experts[None, None, :], route_weight[:, :, None], 0.0),
        axis=1,
    )
    route_high = lax.reduce_precision(route, 8, 7)
    route_low = route - route_high
    packed = jnp.concatenate(
        [my_keys, my_values, route_high.astype(jnp.bfloat16), route_low.astype(jnp.bfloat16)], axis=1
    )
    gathered = gather_rows(packed, ctx_count)
    all_keys = gathered[:, :HEAD_SIZE]
    all_values = gathered[:, HEAD_SIZE : 2 * HEAD_SIZE]
    all_route = gathered[:, 2 * HEAD_SIZE :].astype(jnp.float32)
    all_route = all_route[:, :expert_count] + all_route[:, expert_count:]
    own_route = lax.dynamic_slice_in_dim(all_route, ctx_index * own_experts, own_experts, 1)

    owners = jnp.array(offsets(ctx_count), jnp.int32) ^ ctx_index
    block_ids = jnp.arange(ctx_count, dtype=jnp.int32)
    key_block = jnp.sum(
        jnp.where(owners[:, None] == block_ids[None, :], block_order[None, :], 0), axis=1
    )
    own_block = key_block[0]
    local_rows = jnp.arange(shard_rows, dtype=jnp.int32)
    query_pos = jnp.tile(own_block * shard_rows + local_rows, local_head)
    key_pos = (key_block[:, None] * shard_rows + local_rows[None, :]).reshape(-1)
    query_flat = (
        queries.reshape(shard_rows, local_head, HEAD_SIZE)
        .transpose(1, 0, 2)
        .reshape(local_head * shard_rows, HEAD_SIZE)
    )
    inv_scale = 1.0 / math.sqrt(HEAD_SIZE)
    visible = key_pos[None, :] <= query_pos[:, None]
    scores = (
        lax.dot_general(
            query_flat, all_keys, (((1,), (1,)), ((), ())), preferred_element_type=jnp.float32
        )
        * inv_scale
    )
    scores = jnp.where(visible, scores, MASKED_SCORE)
    newest = jnp.max(scores, axis=1)
    weights = jnp.where(visible, jnp.exp(scores - newest[:, None]), 0.0)
    weight_sum = jnp.sum(weights, axis=1)
    weighted = jnp.dot(weights.astype(jnp.bfloat16), all_values, preferred_element_type=jnp.float32)
    attention = (
        (weighted / weight_sum[:, None])
        .reshape(local_head, shard_rows, HEAD_SIZE)
        .transpose(1, 0, 2)
        .reshape(shard_rows, local_head * HEAD_SIZE)
        .astype(jnp.bfloat16)
    )
    mixed_rows = (residual.astype(jnp.float32) + attention.astype(jnp.float32)).astype(jnp.bfloat16)
    mixed_f = mixed_rows.astype(jnp.float32)
    routed_sum = routed_at_once(
        mixed_rows, norm_gain, own_route, gate_weight, up_weight, down_weight
    )
    return (mixed_f + routed_sum).astype(jnp.bfloat16)


def pack_kernel(head_ref, key_ref, value_ref, ids_ref, route_ref, out_ref, ids, weights, sems):
    columns = pl.ds(pl.multiple_of(head_ref[0] * HEAD_SIZE, HEAD_SIZE), HEAD_SIZE)
    copies = [
        pltpu.make_async_copy(ids_ref, ids, sems.at[0]),
        pltpu.make_async_copy(route_ref, weights, sems.at[1]),
        pltpu.make_async_copy(key_ref.at[:, columns], out_ref.at[:, :HEAD_SIZE], sems.at[2]),
        pltpu.make_async_copy(
            value_ref.at[:, columns], out_ref.at[:, HEAD_SIZE : 2 * HEAD_SIZE], sems.at[3]
        ),
    ]
    for copy in copies:
        copy.start()
    copies[0].wait()
    copies[1].wait()
    rows = out_ref.shape[0]
    line = lax.broadcasted_iota(jnp.int32, (LANES, rows), 0)
    expert = line % ROUTE_LANES
    route = jnp.zeros(line.shape, jnp.float32)
    for i in range(TOPK):
        route = route + jnp.where(ids[i : i + 1, :] == expert, weights[i : i + 1, :], 0.0)
    high = route.astype(jnp.bfloat16).astype(jnp.float32)
    both = jnp.where(line < ROUTE_LANES, high, route - high)
    both = jnp.concatenate([both, jnp.zeros((LANES, LANES - rows), jnp.float32)], axis=1)
    out_ref[:, 2 * HEAD_SIZE :] = jnp.transpose(both)[:rows].astype(jnp.bfloat16)
    copies[2].wait()
    copies[3].wait()


def attention_kernel(place_ref, order_ref, query_ref, packed_ref, residual_ref, out_ref):
    rows = query_ref.shape[0]
    heads = query_ref.shape[1] // HEAD_SIZE
    count = packed_ref.shape[0]
    queries = jnp.concatenate(
        [query_ref[:, h * HEAD_SIZE : (h + 1) * HEAD_SIZE] for h in range(heads)], axis=0
    )
    scores = lax.dot_general(
        queries,
        packed_ref[:, :HEAD_SIZE],
        (((1,), (1,)), ((), ())),
        preferred_element_type=jnp.float32,
    ) * (1.0 / math.sqrt(HEAD_SIZE))
    me = place_ref[0]
    column = lax.broadcasted_iota(jnp.int32, (rows, count), 1)
    key_pos = column % rows
    for i, offset in enumerate(offsets(count // rows)):
        key_pos = key_pos + jnp.where(column // rows == i, order_ref[me ^ offset] * rows, 0)
    query_pos = order_ref[me] * rows + lax.broadcasted_iota(jnp.int32, (rows, count), 0)
    visible = jnp.concatenate([key_pos <= query_pos] * heads, axis=0)
    scores = jnp.where(visible, scores, MASKED_SCORE)
    largest = jnp.max(scores, axis=1, keepdims=True)
    weights = jnp.where(visible, jnp.exp(scores - largest), 0.0)
    weight_sum = jnp.sum(weights, axis=1, keepdims=True)
    weighted = jnp.dot(
        weights.astype(jnp.bfloat16),
        packed_ref[:, HEAD_SIZE : 2 * HEAD_SIZE],
        preferred_element_type=jnp.float32,
    )
    attention = (weighted / weight_sum).astype(jnp.bfloat16)
    for h in range(heads):
        columns = slice(h * HEAD_SIZE, (h + 1) * HEAD_SIZE)
        part = attention[h * rows : (h + 1) * rows].astype(jnp.float32)
        out_ref[:, columns] = (residual_ref[:, columns].astype(jnp.float32) + part).astype(
            jnp.bfloat16
        )


def prepared(blocks, gain_ref):
    rows = jnp.concatenate([block[...] for block in blocks], axis=0).astype(jnp.float32)
    squares = jnp.sum(rows * rows, axis=1, keepdims=True)
    return (rows * gain_ref[...]).astype(jnp.bfloat16), squares


def first_kernel(index_ref, gain_ref, gate_ref, up_ref, *rest):
    out_ref = rest[-1]
    k = index_ref[0]
    size = gate_ref.shape[2]
    rows, squares = prepared(rest[:-1], gain_ref)
    gate = jnp.dot(rows, gate_ref[k], preferred_element_type=jnp.float32)
    out_ref[:, :size] = gate.astype(jnp.bfloat16)
    up = jnp.dot(rows, up_ref[k], preferred_element_type=jnp.float32)
    out_ref[:, size : 2 * size] = up.astype(jnp.bfloat16)
    high = squares.astype(jnp.bfloat16).astype(jnp.float32)
    lane = lax.broadcasted_iota(jnp.int32, (rows.shape[0], LANES), 1)
    out_ref[:, 2 * size :] = jnp.where(lane == 0, high, squares - high).astype(jnp.bfloat16)


def hidden_kernel(places, index_ref, kept_ref, arrived_ref, packed_ref, out_ref):
    size = out_ref.shape[1]
    rows = out_ref.shape[0] // len(places)
    tail = kept_ref[:, 2 * size :].astype(jnp.float32) + arrived_ref[:, 2 * size :].astype(
        jnp.float32
    )
    scale = lax.rsqrt((tail[:, :1] + tail[:, 1:2]) / D + NORM_EPS)
    route = jnp.concatenate(
        [packed_ref[place * rows : (place + 1) * rows, 2 * HEAD_SIZE :] for place in places], axis=0
    ).astype(jnp.float32)
    lane = lax.broadcasted_iota(jnp.int32, route.shape, 1)
    route = jnp.sum(
        jnp.where(lane % ROUTE_LANES == index_ref[0], route, 0.0), axis=1, keepdims=True
    )
    gate = kept_ref[:, :size].astype(jnp.float32) + arrived_ref[:, :size].astype(jnp.float32)
    up = kept_ref[:, size : 2 * size].astype(jnp.float32) + arrived_ref[
        :, size : 2 * size
    ].astype(jnp.float32)
    gate = gate * scale
    up = up * (scale * route)
    out_ref[...] = (gate / (1.0 + jnp.exp(-gate)) * up).astype(jnp.bfloat16)


def own_kernel(index_ref, hidden_ref, down_ref, mixed_ref, *rest):
    out_ref = rest[-1]
    total = mixed_ref[...].astype(jnp.float32) + jnp.dot(
        hidden_ref[...], down_ref[index_ref[0]], preferred_element_type=jnp.float32
    )
    for term in rest[:-1]:
        total = total + term[...].astype(jnp.float32)
    out_ref[...] = total.astype(out_ref.dtype)


def both_kernel(places, mine_ref, other_ref, hidden_ref, other_hidden_ref, down_ref, *rest):
    both = jnp.dot(hidden_ref[...], down_ref[mine_ref[0]], preferred_element_type=jnp.float32)
    both = both + jnp.dot(
        other_hidden_ref[...], down_ref[other_ref[0]], preferred_element_type=jnp.float32
    )
    rows = rest[-1].shape[0]
    for i, out_ref in enumerate(rest[len(places) :]):
        term = both[i * rows : (i + 1) * rows]
        for place, term_ref in zip(places, rest):
            if place == i:
                term = term + term_ref[...].astype(jnp.float32)
        out_ref[...] = term.astype(out_ref.dtype)


class Core:
    def __init__(self):
        self.before = None
        self.also = []

    def __call__(self, kernel, out_shape, *args, held=(), cost=0, scratch=(), space=pltpu.VMEM):
        vmem = pl.BlockSpec(memory_space=pltpu.VMEM)
        specs = [
            pl.BlockSpec(memory_space=pltpu.SMEM if arg.ndim == 1 else space) for arg in args
        ]
        unread = list(held) + ([] if self.before is None else [self.before]) + self.also
        self.also = []
        specs += [vmem] * len(held) + [pl.BlockSpec(memory_space=pl.ANY)] * (len(unread) - len(held))
        read = len(args)
        many = isinstance(out_shape, list)

        def body(*refs):
            kernel(*refs[:read], *refs[read + len(unread) :])

        out = pl.pallas_call(
            body,
            out_shape=out_shape,
            in_specs=specs,
            out_specs=[vmem] * len(out_shape) if many else vmem,
            scratch_shapes=list(scratch),
            compiler_params=pltpu.CompilerParams(vmem_limit_bytes=KERNEL_BYTES),
            cost_estimate=pl.CostEstimate(
                flops=int(cost * COST), bytes_accessed=0, transcendentals=0
            ),
        )(*args, *unread)
        self.before = out[0] if many else out
        return out


def local(
    queries,
    key_rows,
    value_head_rows,
    block_order,
    residual,
    norm_gain,
    expert_ids,
    route_weight,
    gate_weight,
    up_weight,
    down_weight,
):
    rows, features = queries.shape
    ctx_count = lax.axis_size("ctx")
    size = gate_weight.shape[2]
    mine = lax.axis_index("exp").astype(jnp.int32).reshape(1)
    other = 1 - mine
    place = lax.axis_index("ctx").astype(jnp.int32).reshape(1)
    expert = 2 * place + mine
    swap = [(0, 1), (1, 0)]
    gain = norm_gain.reshape(1, features)
    position = {offset: i for i, offset in enumerate(offsets(ctx_count))}
    core = Core()

    def of(shape, dtype=jnp.bfloat16):
        return jax.ShapeDtypeStruct(shape, dtype)

    def hop(block, offset):
        return lax.ppermute(block, "ctx", xor_pairs(ctx_count, offset))

    packed = core(
        pack_kernel,
        of((rows, 2 * HEAD_SIZE + LANES)),
        mine,
        key_rows,
        value_head_rows,
        expert_ids.T,
        route_weight.T,
        cost=PACK_COST,
        space=pl.ANY,
        scratch=(
            pltpu.VMEM((TOPK, rows), jnp.int32),
            pltpu.VMEM((TOPK, rows), jnp.float32),
            pltpu.SemaphoreType.DMA((4,)),
        ),
    )
    packed = gather_rows(packed, ctx_count)
    mixed_rows = core(
        attention_kernel,
        of((rows, features)),
        place,
        block_order,
        queries,
        packed,
        residual,
        held=(gate_weight, up_weight) if HELD else (),
        cost=ATT_COST,
    )

    block = {0: mixed_rows}
    for source, offset in HOPS:
        block[source ^ offset] = hop(block[source], offset)

    kept, arrived, hidden, other_hidden, terms = {}, {}, {}, {}, {}
    for step, i in STEPS:
        chunk = CHUNKS[i % len(CHUNKS)]
        count = len(chunk) * rows
        if step in ("send", "keep"):
            product = core(
                first_kernel,
                of((count, 2 * size + LANES)),
                other if step == "send" else mine,
                gain,
                gate_weight,
                up_weight,
                *[block[offset] for offset in chunk],
                cost=1.2,
            )
            if step == "send":
                arrived[i] = lax.ppermute(product, "exp", swap)
            else:
                kept[i] = product
        elif step == "hidden":
            kernel = functools.partial(hidden_kernel, [position[offset] for offset in chunk])
            hidden[i] = core(kernel, of((count, size)), expert, kept[i], arrived[i], packed, cost=0.4)
            other_hidden[i] = lax.ppermute(hidden[i], "exp", swap)
        elif step == "both":
            shapes = [of((rows, features))] * len(chunk)
            arrivals = [(at, term) for at, o in enumerate(chunk) for term in terms.pop(o, [])]
            kernel = functools.partial(both_kernel, [at for at, _ in arrivals])
            out = core(
                kernel,
                shapes,
                mine, other, hidden[i], other_hidden[i], down_weight,
                *[term for _, term in arrivals],
                cost=1.1,
            )
            for offset, term in zip(chunk, out):
                terms.setdefault(offset ^ SENDS[offset], []).append(hop(term, SENDS[offset]))
        elif step == "wait":
            core.also += terms[0][-i:]
        else:
            ready = [terms[0].pop(0) for _ in range(OWN[step])]
            if step == "own":
                total = core(
                    own_kernel,
                    of((rows, features), jnp.float32),
                    mine, hidden[i], down_weight, mixed_rows, *ready,
                    cost=0.7,
                )
            else:
                total = core(
                    own_kernel,
                    of((rows, features)),
                    other, other_hidden[i], down_weight, total, *ready,
                    cost=0.7,
                )
    return total


def solution(mesh):
    placed = (
        P(("rep", "ctx"), "exp"),
        P(("rep", "ctx"), None),
        P(("rep", "ctx"), None),
        P("rep"),
        P(("rep", "ctx"), "exp"),
        P("exp"),
        P(("rep", "ctx"), None),
        P(("rep", "ctx"), None),
        P("ctx", "exp", None),
        P("ctx", "exp", None),
        P("ctx", None, "exp"),
    )
    small = mesh.shape["exp"] == 2 and mesh.shape["ctx"] == 8
    return jax.shard_map(
        local if small else general, mesh=mesh, in_specs=placed, out_specs=P(("rep", "ctx"), "exp"), check_vma=False
    )
```

```python
import functools
import math

import jax
import jax.numpy as jnp
from jax import lax
from jax.experimental import pallas as pl
from jax.experimental.pallas import tpu as pltpu
from jax.sharding import PartitionSpec as P

D = 4096
QUERY_HEADS = 32
KEY_VALUE_HEADS = 2
HEAD_SIZE = 128
TOPK = 8

MASKED_SCORE = -1e30
NORM_EPS = 1e-06
LANES = 128
KERNEL_BYTES = 16 * 1024 * 1024
ROUTE_LANES = 16
HELD = False
COST = 2e9
PACK_COST = 5
ATT_COST = 5
HOPS = ((0, 4), (0, 1), (4, 2), (4, 1), (6, 1), (0, 2), (2, 1))
CHUNKS = ((0,), (2, 1), (6, 5), (7,), (4,), (3,))
SENDS = {0: 0, 1: 1, 2: 2, 3: 3, 4: 4, 5: 1, 6: 2, 7: 3}
STEPS = (
    ("send", 0),
    ("keep", 0),
    ("send", 1),
    ("hidden", 0),
    ("keep", 1),
    ("send", 2),
    ("both", 0),
    ("hidden", 1),
    ("keep", 2),
    ("send", 3),
    ("both", 1),
    ("hidden", 2),
    ("keep", 3),
    ("hidden", 3),
    ("send", 4),
    ("both", 2),
    ("both", 3),
    ("keep", 4),
    ("send", 5),
    ("hidden", 4),
    ("keep", 5),
    ("both", 4),
    ("hidden", 5),
    ("both", 5),
    ("sum", 0),
)
def xor_pairs(count, bit):
    return [(i, i ^ bit) for i in range(count)]


def bits_of(count):
    bits = []
    bit = count // 2
    while bit:
        bits.append(bit)
        bit //= 2
    return bits


def gather_rows(block, count):
    for bit in bits_of(count):
        block = jnp.concatenate([block, lax.ppermute(block, "ctx", xor_pairs(count, bit))], axis=0)
    return block


def offsets(count):
    found = [0]
    for bit in bits_of(count):
        found = found + [offset ^ bit for offset in found]
    return found


def scatter_sums(partial, count):
    for bit in reversed(bits_of(count)):
        half = partial.shape[0] // 2
        arrived = lax.ppermute(partial[half:].astype(jnp.bfloat16), "ctx", xor_pairs(count, bit))
        partial = partial[:half] + arrived.astype(jnp.float32)
    return partial


def routed_at_once(mixed_rows, norm_gain, own_route, gate_weight, up_weight, down_weight):
    ctx_count = lax.axis_size("ctx")
    own_experts, _, hidden_size = gate_weight.shape
    mixed_f = mixed_rows.astype(jnp.float32)
    square_sum = lax.psum(jnp.sum(mixed_f * mixed_f, axis=1), "exp")
    normed = (mixed_f * lax.rsqrt(square_sum[:, None] / D + NORM_EPS) * norm_gain[None, :]).astype(
        jnp.bfloat16
    )
    all_normed = gather_rows(normed, ctx_count)
    share = all_normed.shape[0] // lax.axis_size("exp")
    terms = []
    for k in range(own_experts):
        for weight in (gate_weight, up_weight):
            term = jnp.dot(all_normed, weight[k], preferred_element_type=jnp.float32)
            terms.append(term.astype(jnp.bfloat16))
    sums = lax.psum_scatter(
        jnp.concatenate(terms, axis=1), "exp", scatter_dimension=0, tiled=True
    ).astype(jnp.float32)
    my_route = lax.dynamic_slice_in_dim(own_route, lax.axis_index("exp") * share, share, 0)
    pieces = []
    for k in range(own_experts):
        gate_sum = sums[:, 2 * k * hidden_size : (2 * k + 1) * hidden_size]
        up_sum = sums[:, (2 * k + 1) * hidden_size : (2 * k + 2) * hidden_size]
        pieces.append((jax.nn.silu(gate_sum) * up_sum * my_route[:, k : k + 1]).astype(jnp.bfloat16))
    hidden = lax.all_gather(jnp.concatenate(pieces, axis=1), "exp", axis=0, tiled=True)
    down = down_weight.reshape(own_experts * hidden_size, down_weight.shape[2])
    partial = jnp.dot(hidden, down, preferred_element_type=jnp.float32)
    return scatter_sums(partial, ctx_count)


def general(
    queries,
    key_rows,
    value_head_rows,
    block_order,
    residual,
    norm_gain,
    expert_ids,
    route_weight,
    gate_weight,
    up_weight,
    down_weight,
):
    shard_rows = queries.shape[0]
    ctx_count = lax.axis_size("ctx")
    local_head = queries.shape[1] // HEAD_SIZE
    expert_index = lax.axis_index("exp")
    ctx_index = lax.axis_index("ctx")
    own_experts = gate_weight.shape[0]
    expert_count = ctx_count * own_experts

    key_value_head = expert_index * local_head // (QUERY_HEADS // KEY_VALUE_HEADS)
    my_keys = lax.dynamic_slice_in_dim(key_rows, key_value_head * HEAD_SIZE, HEAD_SIZE, 1)
    my_values = lax.dynamic_slice_in_dim(value_head_rows, key_value_head * HEAD_SIZE, HEAD_SIZE, 1)
    experts = jnp.arange(expert_count, dtype=jnp.int32)
    route = jnp.sum(
        jnp.where(expert_ids[:, :, None] == experts[None, None, :], route_weight[:, :, None], 0.0),
        axis=1,
    )
    route_high = lax.reduce_precision(route, 8, 7)
    route_low = route - route_high
    packed = jnp.concatenate(
        [my_keys, my_values, route_high.astype(jnp.bfloat16), route_low.astype(jnp.bfloat16)], axis=1
    )
    gathered = gather_rows(packed, ctx_count)
    all_keys = gathered[:, :HEAD_SIZE]
    all_values = gathered[:, HEAD_SIZE : 2 * HEAD_SIZE]
    all_route = gathered[:, 2 * HEAD_SIZE :].astype(jnp.float32)
    all_route = all_route[:, :expert_count] + all_route[:, expert_count:]
    own_route = lax.dynamic_slice_in_dim(all_route, ctx_index * own_experts, own_experts, 1)

    owners = jnp.array(offsets(ctx_count), jnp.int32) ^ ctx_index
    block_ids = jnp.arange(ctx_count, dtype=jnp.int32)
    key_block = jnp.sum(
        jnp.where(owners[:, None] == block_ids[None, :], block_order[None, :], 0), axis=1
    )
    own_block = key_block[0]
    local_rows = jnp.arange(shard_rows, dtype=jnp.int32)
    query_pos = jnp.tile(own_block * shard_rows + local_rows, local_head)
    key_pos = (key_block[:, None] * shard_rows + local_rows[None, :]).reshape(-1)
    query_flat = (
        queries.reshape(shard_rows, local_head, HEAD_SIZE)
        .transpose(1, 0, 2)
        .reshape(local_head * shard_rows, HEAD_SIZE)
    )
    inv_scale = 1.0 / math.sqrt(HEAD_SIZE)
    visible = key_pos[None, :] <= query_pos[:, None]
    scores = (
        lax.dot_general(
            query_flat, all_keys, (((1,), (1,)), ((), ())), preferred_element_type=jnp.float32
        )
        * inv_scale
    )
    scores = jnp.where(visible, scores, MASKED_SCORE)
    newest = jnp.max(scores, axis=1)
    weights = jnp.where(visible, jnp.exp(scores - newest[:, None]), 0.0)
    weight_sum = jnp.sum(weights, axis=1)
    weighted = jnp.dot(weights.astype(jnp.bfloat16), all_values, preferred_element_type=jnp.float32)
    attention = (
        (weighted / weight_sum[:, None])
        .reshape(local_head, shard_rows, HEAD_SIZE)
        .transpose(1, 0, 2)
        .reshape(shard_rows, local_head * HEAD_SIZE)
        .astype(jnp.bfloat16)
    )
    mixed_rows = (residual.astype(jnp.float32) + attention.astype(jnp.float32)).astype(jnp.bfloat16)
    mixed_f = mixed_rows.astype(jnp.float32)
    routed_sum = routed_at_once(
        mixed_rows, norm_gain, own_route, gate_weight, up_weight, down_weight
    )
    return (mixed_f + routed_sum).astype(jnp.bfloat16)


def pack_kernel(key_ref, value_ref, high_ref, low_ref, out_ref):
    out_ref[:, :HEAD_SIZE] = key_ref[...]
    out_ref[:, HEAD_SIZE : 2 * HEAD_SIZE] = value_ref[...]
    out_ref[:, 2 * HEAD_SIZE : 2 * HEAD_SIZE + ROUTE_LANES] = high_ref[...]
    out_ref[:, 2 * HEAD_SIZE + ROUTE_LANES : 2 * HEAD_SIZE + 2 * ROUTE_LANES] = low_ref[...]


def attention_kernel(place_ref, order_ref, query_ref, packed_ref, residual_ref, out_ref):
    rows = query_ref.shape[0]
    heads = query_ref.shape[1] // HEAD_SIZE
    count = packed_ref.shape[0]
    queries = jnp.concatenate(
        [query_ref[:, h * HEAD_SIZE : (h + 1) * HEAD_SIZE] for h in range(heads)], axis=0
    )
    scores = lax.dot_general(
        queries,
        packed_ref[:, :HEAD_SIZE],
        (((1,), (1,)), ((), ())),
        preferred_element_type=jnp.float32,
    ) * (1.0 / math.sqrt(HEAD_SIZE))
    me = place_ref[0]
    column = lax.broadcasted_iota(jnp.int32, (rows, count), 1)
    key_pos = column % rows
    for i, offset in enumerate(offsets(count // rows)):
        key_pos = key_pos + jnp.where(column // rows == i, order_ref[me ^ offset] * rows, 0)
    query_pos = order_ref[me] * rows + lax.broadcasted_iota(jnp.int32, (rows, count), 0)
    visible = jnp.concatenate([key_pos <= query_pos] * heads, axis=0)
    scores = jnp.where(visible, scores, MASKED_SCORE)
    largest = jnp.max(scores, axis=1, keepdims=True)
    weights = jnp.where(visible, jnp.exp(scores - largest), 0.0)
    weight_sum = jnp.sum(weights, axis=1, keepdims=True)
    weighted = jnp.dot(
        weights.astype(jnp.bfloat16),
        packed_ref[:, HEAD_SIZE : 2 * HEAD_SIZE],
        preferred_element_type=jnp.float32,
    )
    attention = (weighted / weight_sum).astype(jnp.bfloat16)
    for h in range(heads):
        columns = slice(h * HEAD_SIZE, (h + 1) * HEAD_SIZE)
        part = attention[h * rows : (h + 1) * rows].astype(jnp.float32)
        out_ref[:, columns] = (residual_ref[:, columns].astype(jnp.float32) + part).astype(
            jnp.bfloat16
        )


def copy_kernel(block_ref, out_ref):
    out_ref[...] = block_ref[...]


def product(rows, weight):
    count = rows.shape[0]
    if count < LANES:
        rows = jnp.concatenate([rows, rows], axis=0)
    return jnp.dot(rows, weight, preferred_element_type=jnp.float32)[:count]


def prepared(blocks, gain_ref):
    rows = jnp.concatenate([block[...] for block in blocks], axis=0).astype(jnp.float32)
    squares = jnp.sum(rows * rows, axis=1, keepdims=True)
    return (rows * gain_ref[...]).astype(jnp.bfloat16), squares


def first_kernel(index_ref, gain_ref, gate_ref, up_ref, *rest):
    out_ref = rest[-1]
    k = index_ref[0]
    size = gate_ref.shape[2]
    rows, squares = prepared(rest[:-1], gain_ref)
    gate = product(rows, gate_ref[k])
    out_ref[:, :size] = gate.astype(jnp.bfloat16)
    up = product(rows, up_ref[k])
    out_ref[:, size : 2 * size] = up.astype(jnp.bfloat16)
    high = squares.astype(jnp.bfloat16).astype(jnp.float32)
    lane = lax.broadcasted_iota(jnp.int32, (rows.shape[0], LANES), 1)
    out_ref[:, 2 * size :] = jnp.where(lane == 0, high, squares - high).astype(jnp.bfloat16)


def hidden_kernel(places, index_ref, kept_ref, arrived_ref, packed_ref, out_ref):
    size = out_ref.shape[1]
    rows = out_ref.shape[0] // len(places)
    tail = kept_ref[:, 2 * size :].astype(jnp.float32) + arrived_ref[:, 2 * size :].astype(
        jnp.float32
    )
    scale = lax.rsqrt((tail[:, :1] + tail[:, 1:2]) / D + NORM_EPS)
    route = jnp.concatenate(
        [packed_ref[place * rows : (place + 1) * rows, 2 * HEAD_SIZE :] for place in places], axis=0
    ).astype(jnp.float32)
    lane = lax.broadcasted_iota(jnp.int32, route.shape, 1)
    named = (lane == index_ref[0]) | (lane == index_ref[0] + ROUTE_LANES)
    route = jnp.sum(jnp.where(named, route, 0.0), axis=1, keepdims=True)
    gate = kept_ref[:, :size].astype(jnp.float32) + arrived_ref[:, :size].astype(jnp.float32)
    up = kept_ref[:, size : 2 * size].astype(jnp.float32) + arrived_ref[
        :, size : 2 * size
    ].astype(jnp.float32)
    gate = gate * scale
    up = up * (scale * route)
    out_ref[...] = (gate / (1.0 + jnp.exp(-gate)) * up).astype(jnp.bfloat16)


def sum_kernel(mixed_ref, *rest):
    total = mixed_ref[...].astype(jnp.float32)
    for term_ref in rest[:-1]:
        total = total + term_ref[...].astype(jnp.float32)
    rest[-1][...] = total.astype(rest[-1].dtype)


def both_kernel(places, mine_ref, other_ref, hidden_ref, other_hidden_ref, down_ref, *rest):
    both = product(hidden_ref[...], down_ref[mine_ref[0]])
    both = both + product(other_hidden_ref[...], down_ref[other_ref[0]])
    rows = rest[-1].shape[0]
    for i, out_ref in enumerate(rest[len(places) :]):
        term = both[i * rows : (i + 1) * rows]
        for place, term_ref in zip(places, rest):
            if place == i:
                term = term + term_ref[...].astype(jnp.float32)
        out_ref[...] = term.astype(out_ref.dtype)


class Core:
    def __init__(self):
        self.before = None
        self.also = []

    def __call__(self, kernel, out_shape, *args, held=(), cost=0):
        vmem = pl.BlockSpec(memory_space=pltpu.VMEM)
        specs = [
            pl.BlockSpec(memory_space=pltpu.SMEM) if arg.ndim == 1 else vmem for arg in args
        ]
        unread = list(held) + ([] if self.before is None else [self.before]) + self.also
        self.also = []
        specs += [vmem] * len(held) + [pl.BlockSpec(memory_space=pl.ANY)] * (len(unread) - len(held))
        read = len(args)
        many = isinstance(out_shape, list)

        def body(*refs):
            kernel(*refs[:read], *refs[read + len(unread) :])

        out = pl.pallas_call(
            body,
            out_shape=out_shape,
            in_specs=specs,
            out_specs=[vmem] * len(out_shape) if many else vmem,
            compiler_params=pltpu.CompilerParams(vmem_limit_bytes=KERNEL_BYTES),
            cost_estimate=pl.CostEstimate(
                flops=int(cost * COST), bytes_accessed=0, transcendentals=0
            ),
        )(*args, *unread)
        self.before = out[0] if many else out
        return out


def local(
    queries,
    key_rows,
    value_head_rows,
    block_order,
    residual,
    norm_gain,
    expert_ids,
    route_weight,
    gate_weight,
    up_weight,
    down_weight,
):
    rows, features = queries.shape
    ctx_count = lax.axis_size("ctx")
    size = gate_weight.shape[2]
    mine = lax.axis_index("exp").astype(jnp.int32).reshape(1)
    other = 1 - mine
    place = lax.axis_index("ctx").astype(jnp.int32).reshape(1)
    expert = 2 * place + mine
    swap = [(0, 1), (1, 0)]
    gain = norm_gain.reshape(1, features)
    position = {offset: i for i, offset in enumerate(offsets(ctx_count))}
    core = Core()

    def of(shape, dtype=jnp.bfloat16):
        return jax.ShapeDtypeStruct(shape, dtype)

    def hop(block, offset):
        return lax.ppermute(block, "ctx", xor_pairs(ctx_count, offset))

    columns = mine[0] * HEAD_SIZE
    experts = jnp.arange(ROUTE_LANES, dtype=jnp.int32)
    named = expert_ids[:, :, None] == experts[None, None, :]
    route = jnp.sum(jnp.where(named, route_weight[:, :, None], 0.0), axis=1)
    high = lax.reduce_precision(route, 8, 7)
    packed = core(
        pack_kernel,
        of((rows, 2 * HEAD_SIZE + LANES)),
        lax.dynamic_slice_in_dim(key_rows, columns, HEAD_SIZE, 1),
        lax.dynamic_slice_in_dim(value_head_rows, columns, HEAD_SIZE, 1),
        high.astype(jnp.bfloat16),
        (route - high).astype(jnp.bfloat16),
        cost=PACK_COST,
    )
    packed = gather_rows(packed, ctx_count)
    mixed_rows = core(
        attention_kernel,
        of((rows, features)),
        place,
        block_order,
        queries,
        packed,
        residual,
        held=(gate_weight, up_weight) if HELD else (),
        cost=ATT_COST,
    )

    block = {0: mixed_rows}
    for source, offset in HOPS:
        block[source ^ offset] = hop(block[source], offset)

    kept, arrived, hidden, other_hidden, terms = {}, {}, {}, {}, {}
    for step, i in STEPS:
        if step == "hop":
            source, offset = i
            again = core(copy_kernel, of((rows, features)), block[source], cost=0.2)
            block[source ^ offset] = hop(again, offset)
            continue
        if step == "sum":
            total = core(sum_kernel, of((rows, features)), mixed_rows, *terms[0])
            continue
        if step == "pin":
            core.also.append(other_hidden[i])
            continue
        if step == "on":
            source, offset = i
            block[source ^ offset] = hop(block[source], offset)
            continue
        chunk = CHUNKS[i % len(CHUNKS)]
        count = len(chunk) * rows
        if step in ("send", "keep"):
            product = core(
                first_kernel,
                of((count, 2 * size + LANES)),
                other if step == "send" else mine,
                gain,
                gate_weight,
                up_weight,
                *[block[offset] for offset in chunk],
                cost=1.2,
            )
            if step == "send":
                arrived[i] = lax.ppermute(product, "exp", swap)
            else:
                kept[i] = product
        elif step == "hidden":
            kernel = functools.partial(hidden_kernel, [position[offset] for offset in chunk])
            hidden[i] = core(kernel, of((count, size)), expert, kept[i], arrived[i], packed, cost=0.4)
            other_hidden[i] = lax.ppermute(hidden[i], "exp", swap)
        else:
            shapes = [of((rows, features), jnp.bfloat16 if o else jnp.float32) for o in chunk]
            arrivals = [(at, term) for at, o in enumerate(chunk) for term in terms.pop(o, [])]
            kernel = functools.partial(both_kernel, [at for at, _ in arrivals])
            out = core(
                kernel,
                shapes,
                mine, other, hidden[i], other_hidden[i], down_weight,
                *[term for _, term in arrivals],
                cost=1.1,
            )
            for offset, term in zip(chunk, out):
                term = hop(term, SENDS[offset]) if offset else term
                terms.setdefault(offset ^ SENDS[offset], []).append(term)
    return total


def solution(mesh):
    placed = (
        P(("rep", "ctx"), "exp"),
        P(("rep", "ctx"), None),
        P(("rep", "ctx"), None),
        P("rep"),
        P(("rep", "ctx"), "exp"),
        P("exp"),
        P(("rep", "ctx"), None),
        P(("rep", "ctx"), None),
        P("ctx", "exp", None),
        P("ctx", "exp", None),
        P("ctx", None, "exp"),
    )
    small = mesh.shape["exp"] == 2 and mesh.shape["ctx"] == 8
    return jax.shard_map(
        local if small else general, mesh=mesh, in_specs=placed, out_specs=P(("rep", "ctx"), "exp"), check_vma=False
    )
```

```python
import functools
import math

import jax
import jax.numpy as jnp
from jax import lax
from jax.experimental import pallas as pl
from jax.experimental.pallas import tpu as pltpu
from jax.sharding import PartitionSpec as P

D = 4096
QUERY_HEADS = 32
KEY_VALUE_HEADS = 2
HEAD_SIZE = 128
TOPK = 8

MASKED_SCORE = -1e30
NORM_EPS = 1e-06
LANES = 128
KERNEL_BYTES = 16 * 1024 * 1024
EXPERT_ROWS = 16
HELD = False
COST = 2e9
FIRST_COST = 1.2
HIDDEN_COST = 0.4
BOTH_COST = 1.1
PACK_COST = 10
ATT_COST = 5
HOPS = ((0, 4), (0, 1), (4, 2), (4, 1), (6, 1), (0, 2), (2, 1))
COSTS = {}
LATER = (2,)
CHUNKS = ((0,), (2, 1), (6, 5), (7,), (4,), (3,))
SENDS = {0: 0, 1: 1, 2: 2, 3: 3, 4: 4, 5: 1, 6: 2, 7: 3}
STEPS = (
    ("send", 0),
    ("keep", 0),
    ("send", 1),
    ("hidden", 0),
    ("keep", 1),
    ("send", 2),
    ("both", 0),
    ("hidden", 1),
    ("keep", 2),
    ("send", 3),
    ("hidden", 2),
    ("both", 1),
    ("keep", 3),
    ("hidden", 3),
    ("send", 4),
    ("both", 2),
    ("both", 3),
    ("got", 1),
    ("got", 2),
    ("keep", 4),
    ("hidden", 4),
    ("send", 5),
    ("keep", 5),
    ("both", 4),
    ("hidden", 5),
    ("both", 5),
    ("sum", 0),
)
def xor_pairs(count, bit):
    return [(i, i ^ bit) for i in range(count)]


def bits_of(count):
    bits = []
    bit = count // 2
    while bit:
        bits.append(bit)
        bit //= 2
    return bits


def gather_rows(block, count):
    for bit in bits_of(count):
        block = jnp.concatenate([block, lax.ppermute(block, "ctx", xor_pairs(count, bit))], axis=0)
    return block


def offsets(count):
    found = [0]
    for bit in bits_of(count):
        found = found + [offset ^ bit for offset in found]
    return found


def scatter_sums(partial, count):
    for bit in reversed(bits_of(count)):
        half = partial.shape[0] // 2
        arrived = lax.ppermute(partial[half:].astype(jnp.bfloat16), "ctx", xor_pairs(count, bit))
        partial = partial[:half] + arrived.astype(jnp.float32)
    return partial


def routed_at_once(mixed_rows, norm_gain, own_route, gate_weight, up_weight, down_weight):
    ctx_count = lax.axis_size("ctx")
    own_experts, _, hidden_size = gate_weight.shape
    mixed_f = mixed_rows.astype(jnp.float32)
    square_sum = lax.psum(jnp.sum(mixed_f * mixed_f, axis=1), "exp")
    normed = (mixed_f * lax.rsqrt(square_sum[:, None] / D + NORM_EPS) * norm_gain[None, :]).astype(
        jnp.bfloat16
    )
    all_normed = gather_rows(normed, ctx_count)
    share = all_normed.shape[0] // lax.axis_size("exp")
    terms = []
    for k in range(own_experts):
        for weight in (gate_weight, up_weight):
            term = jnp.dot(all_normed, weight[k], preferred_element_type=jnp.float32)
            terms.append(term.astype(jnp.bfloat16))
    sums = lax.psum_scatter(
        jnp.concatenate(terms, axis=1), "exp", scatter_dimension=0, tiled=True
    ).astype(jnp.float32)
    my_route = lax.dynamic_slice_in_dim(own_route, lax.axis_index("exp") * share, share, 0)
    pieces = []
    for k in range(own_experts):
        gate_sum = sums[:, 2 * k * hidden_size : (2 * k + 1) * hidden_size]
        up_sum = sums[:, (2 * k + 1) * hidden_size : (2 * k + 2) * hidden_size]
        pieces.append((jax.nn.silu(gate_sum) * up_sum * my_route[:, k : k + 1]).astype(jnp.bfloat16))
    hidden = lax.all_gather(jnp.concatenate(pieces, axis=1), "exp", axis=0, tiled=True)
    down = down_weight.reshape(own_experts * hidden_size, down_weight.shape[2])
    partial = jnp.dot(hidden, down, preferred_element_type=jnp.float32)
    return scatter_sums(partial, ctx_count)


def general(
    queries,
    key_rows,
    value_head_rows,
    block_order,
    residual,
    norm_gain,
    expert_ids,
    route_weight,
    gate_weight,
    up_weight,
    down_weight,
):
    shard_rows = queries.shape[0]
    ctx_count = lax.axis_size("ctx")
    local_head = queries.shape[1] // HEAD_SIZE
    expert_index = lax.axis_index("exp")
    ctx_index = lax.axis_index("ctx")
    own_experts = gate_weight.shape[0]
    expert_count = ctx_count * own_experts

    key_value_head = expert_index * local_head // (QUERY_HEADS // KEY_VALUE_HEADS)
    my_keys = lax.dynamic_slice_in_dim(key_rows, key_value_head * HEAD_SIZE, HEAD_SIZE, 1)
    my_values = lax.dynamic_slice_in_dim(value_head_rows, key_value_head * HEAD_SIZE, HEAD_SIZE, 1)
    experts = jnp.arange(expert_count, dtype=jnp.int32)
    route = jnp.sum(
        jnp.where(expert_ids[:, :, None] == experts[None, None, :], route_weight[:, :, None], 0.0),
        axis=1,
    )
    route_high = lax.reduce_precision(route, 8, 7)
    route_low = route - route_high
    packed = jnp.concatenate(
        [my_keys, my_values, route_high.astype(jnp.bfloat16), route_low.astype(jnp.bfloat16)], axis=1
    )
    gathered = gather_rows(packed, ctx_count)
    all_keys = gathered[:, :HEAD_SIZE]
    all_values = gathered[:, HEAD_SIZE : 2 * HEAD_SIZE]
    all_route = gathered[:, 2 * HEAD_SIZE :].astype(jnp.float32)
    all_route = all_route[:, :expert_count] + all_route[:, expert_count:]
    own_route = lax.dynamic_slice_in_dim(all_route, ctx_index * own_experts, own_experts, 1)

    owners = jnp.array(offsets(ctx_count), jnp.int32) ^ ctx_index
    block_ids = jnp.arange(ctx_count, dtype=jnp.int32)
    key_block = jnp.sum(
        jnp.where(owners[:, None] == block_ids[None, :], block_order[None, :], 0), axis=1
    )
    own_block = key_block[0]
    local_rows = jnp.arange(shard_rows, dtype=jnp.int32)
    query_pos = jnp.tile(own_block * shard_rows + local_rows, local_head)
    key_pos = (key_block[:, None] * shard_rows + local_rows[None, :]).reshape(-1)
    query_flat = (
        queries.reshape(shard_rows, local_head, HEAD_SIZE)
        .transpose(1, 0, 2)
        .reshape(local_head * shard_rows, HEAD_SIZE)
    )
    inv_scale = 1.0 / math.sqrt(HEAD_SIZE)
    visible = key_pos[None, :] <= query_pos[:, None]
    scores = (
        lax.dot_general(
            query_flat, all_keys, (((1,), (1,)), ((), ())), preferred_element_type=jnp.float32
        )
        * inv_scale
    )
    scores = jnp.where(visible, scores, MASKED_SCORE)
    newest = jnp.max(scores, axis=1)
    weights = jnp.where(visible, jnp.exp(scores - newest[:, None]), 0.0)
    weight_sum = jnp.sum(weights, axis=1)
    weighted = jnp.dot(weights.astype(jnp.bfloat16), all_values, preferred_element_type=jnp.float32)
    attention = (
        (weighted / weight_sum[:, None])
        .reshape(local_head, shard_rows, HEAD_SIZE)
        .transpose(1, 0, 2)
        .reshape(shard_rows, local_head * HEAD_SIZE)
        .astype(jnp.bfloat16)
    )
    mixed_rows = (residual.astype(jnp.float32) + attention.astype(jnp.float32)).astype(jnp.bfloat16)
    mixed_f = mixed_rows.astype(jnp.float32)
    routed_sum = routed_at_once(
        mixed_rows, norm_gain, own_route, gate_weight, up_weight, down_weight
    )
    return (mixed_f + routed_sum).astype(jnp.bfloat16)


def pack_kernel(key_ref, value_ref, route_ref, out_ref):
    rows = key_ref.shape[0]
    out_ref[:rows] = key_ref[...]
    out_ref[rows : 2 * rows] = value_ref[...]
    out_ref[2 * rows :] = route_ref[...]


def attention_kernel(place_ref, order_ref, query_ref, packed_ref, residual_ref, out_ref):
    rows = query_ref.shape[0]
    heads = query_ref.shape[1] // HEAD_SIZE
    block = 2 * rows + EXPERT_ROWS
    starts = range(0, packed_ref.shape[0], block)
    count = len(starts) * rows
    keys = jnp.concatenate([packed_ref[i : i + rows] for i in starts], axis=0)
    values = jnp.concatenate([packed_ref[i + rows : i + 2 * rows] for i in starts], axis=0)
    queries = jnp.concatenate(
        [query_ref[:, h * HEAD_SIZE : (h + 1) * HEAD_SIZE] for h in range(heads)], axis=0
    )
    scores = lax.dot_general(
        queries,
        keys,
        (((1,), (1,)), ((), ())),
        preferred_element_type=jnp.float32,
    ) * (1.0 / math.sqrt(HEAD_SIZE))
    me = place_ref[0]
    column = lax.broadcasted_iota(jnp.int32, (rows, count), 1)
    key_pos = column % rows
    for i, offset in enumerate(offsets(count // rows)):
        key_pos = key_pos + jnp.where(column // rows == i, order_ref[me ^ offset] * rows, 0)
    query_pos = order_ref[me] * rows + lax.broadcasted_iota(jnp.int32, (rows, count), 0)
    visible = jnp.concatenate([key_pos <= query_pos] * heads, axis=0)
    scores = jnp.where(visible, scores, MASKED_SCORE)
    largest = jnp.max(scores, axis=1, keepdims=True)
    weights = jnp.where(visible, jnp.exp(scores - largest), 0.0)
    weight_sum = jnp.sum(weights, axis=1, keepdims=True)
    weighted = jnp.dot(
        weights.astype(jnp.bfloat16),
        values,
        preferred_element_type=jnp.float32,
    )
    attention = (weighted / weight_sum).astype(jnp.bfloat16)
    for h in range(heads):
        columns = slice(h * HEAD_SIZE, (h + 1) * HEAD_SIZE)
        part = attention[h * rows : (h + 1) * rows].astype(jnp.float32)
        out_ref[:, columns] = (residual_ref[:, columns].astype(jnp.float32) + part).astype(
            jnp.bfloat16
        )


def copy_kernel(block_ref, out_ref):
    out_ref[...] = block_ref[...]


def product(rows, weight):
    count = rows.shape[0]
    if count < LANES:
        rows = jnp.concatenate([rows, rows], axis=0)
    return jnp.dot(rows, weight, preferred_element_type=jnp.float32)[:count]


def prepared(blocks, gain_ref):
    rows = jnp.concatenate([block[...] for block in blocks], axis=0).astype(jnp.float32)
    squares = jnp.sum(rows * rows, axis=1, keepdims=True)
    return (rows * gain_ref[...]).astype(jnp.bfloat16), squares


def first_kernel(index_ref, gain_ref, gate_ref, up_ref, *rest):
    out_ref = rest[-1]
    k = index_ref[0]
    size = gate_ref.shape[2]
    rows, squares = prepared(rest[:-1], gain_ref)
    gate = product(rows, gate_ref[k])
    out_ref[:, :size] = gate.astype(jnp.bfloat16)
    up = product(rows, up_ref[k])
    out_ref[:, size : 2 * size] = up.astype(jnp.bfloat16)
    high = squares.astype(jnp.bfloat16).astype(jnp.float32)
    lane = lax.broadcasted_iota(jnp.int32, (rows.shape[0], LANES), 1)
    out_ref[:, 2 * size :] = jnp.where(lane == 0, high, squares - high).astype(jnp.bfloat16)


def hidden_kernel(places, index_ref, kept_ref, arrived_ref, packed_ref, out_ref):
    size = out_ref.shape[1]
    rows = out_ref.shape[0] // len(places)
    tail = kept_ref[:, 2 * size :].astype(jnp.float32) + arrived_ref[:, 2 * size :].astype(
        jnp.float32
    )
    scale = lax.rsqrt((tail[:, :1] + tail[:, 1:2]) / D + NORM_EPS)
    block = 2 * rows + EXPERT_ROWS
    expert = lax.broadcasted_iota(jnp.int32, (EXPERT_ROWS, 2 * rows), 0)
    row = lax.broadcasted_iota(jnp.int32, (rows, 2 * rows), 0)
    lane = lax.broadcasted_iota(jnp.int32, (rows, 2 * rows), 1)
    columns = []
    for place in places:
        part = packed_ref[place * block + 2 * rows : (place + 1) * block].astype(jnp.float32)
        line = jnp.sum(jnp.where(expert == index_ref[0], part, 0.0), axis=0, keepdims=True)
        columns.append(jnp.sum(jnp.where(lane % rows == row, line, 0.0), axis=1, keepdims=True))
    route = jnp.concatenate(columns, axis=0)
    gate = kept_ref[:, :size].astype(jnp.float32) + arrived_ref[:, :size].astype(jnp.float32)
    up = kept_ref[:, size : 2 * size].astype(jnp.float32) + arrived_ref[
        :, size : 2 * size
    ].astype(jnp.float32)
    gate = gate * scale
    up = up * (scale * route)
    out_ref[...] = (gate / (1.0 + jnp.exp(-gate)) * up).astype(jnp.bfloat16)


def sum_kernel(mixed_ref, *rest):
    total = mixed_ref[...].astype(jnp.float32)
    for term_ref in rest[:-1]:
        total = total + term_ref[...].astype(jnp.float32)
    rest[-1][...] = total.astype(rest[-1].dtype)


def both_kernel(places, mine_ref, other_ref, hidden_ref, other_hidden_ref, down_ref, *rest):
    both = product(hidden_ref[...], down_ref[mine_ref[0]])
    both = both + product(other_hidden_ref[...], down_ref[other_ref[0]])
    rows = rest[-1].shape[0]
    for i, out_ref in enumerate(rest[len(places) :]):
        term = both[i * rows : (i + 1) * rows]
        for place, term_ref in zip(places, rest):
            if place == i:
                term = term + term_ref[...].astype(jnp.float32)
        out_ref[...] = term.astype(out_ref.dtype)


class Core:
    def __init__(self):
        self.before = None
        self.also = []

    def __call__(self, kernel, out_shape, *args, held=(), cost=0):
        vmem = pl.BlockSpec(memory_space=pltpu.VMEM)
        specs = [
            pl.BlockSpec(memory_space=pltpu.SMEM) if arg.ndim == 1 else vmem for arg in args
        ]
        unread = list(held) + ([] if self.before is None else [self.before]) + self.also
        self.also = []
        specs += [vmem] * len(held) + [pl.BlockSpec(memory_space=pl.ANY)] * (len(unread) - len(held))
        read = len(args)
        many = isinstance(out_shape, list)

        def body(*refs):
            kernel(*refs[:read], *refs[read + len(unread) :])

        out = pl.pallas_call(
            body,
            out_shape=out_shape,
            in_specs=specs,
            out_specs=[vmem] * len(out_shape) if many else vmem,
            compiler_params=pltpu.CompilerParams(vmem_limit_bytes=KERNEL_BYTES),
            cost_estimate=pl.CostEstimate(
                flops=int(cost * COST), bytes_accessed=0, transcendentals=0
            ),
        )(*args, *unread)
        self.before = out[0] if many else out
        return out


def local(
    queries,
    key_rows,
    value_head_rows,
    block_order,
    residual,
    norm_gain,
    expert_ids,
    route_weight,
    gate_weight,
    up_weight,
    down_weight,
):
    rows, features = queries.shape
    ctx_count = lax.axis_size("ctx")
    size = gate_weight.shape[2]
    mine = lax.axis_index("exp").astype(jnp.int32).reshape(1)
    other = 1 - mine
    place = lax.axis_index("ctx").astype(jnp.int32).reshape(1)
    expert = 2 * place + mine
    swap = [(0, 1), (1, 0)]
    gain = norm_gain.reshape(1, features)
    position = {offset: i for i, offset in enumerate(offsets(ctx_count))}
    core = Core()

    def of(shape, dtype=jnp.bfloat16):
        return jax.ShapeDtypeStruct(shape, dtype)

    def hop(block, offset):
        return lax.ppermute(block, "ctx", xor_pairs(ctx_count, offset))

    columns = mine[0] * HEAD_SIZE
    experts = jnp.arange(EXPERT_ROWS, dtype=jnp.int32)
    named = expert_ids.T[:, None, :] == experts[None, :, None]
    route = jnp.sum(jnp.where(named, route_weight.T[:, None, :], 0.0), axis=0)
    high = lax.reduce_precision(route, 8, 7)
    packed = core(
        pack_kernel,
        of((2 * rows + EXPERT_ROWS, HEAD_SIZE)),
        lax.dynamic_slice_in_dim(key_rows, columns, HEAD_SIZE, 1),
        lax.dynamic_slice_in_dim(value_head_rows, columns, HEAD_SIZE, 1),
        jnp.concatenate([high, route - high], axis=1).astype(jnp.bfloat16),
        cost=PACK_COST,
    )
    packed = gather_rows(packed, ctx_count)
    mixed_rows = core(
        attention_kernel,
        of((rows, features)),
        place,
        block_order,
        queries,
        packed,
        residual,
        held=(gate_weight, up_weight) if HELD else (),
        cost=ATT_COST,
    )

    block = {0: mixed_rows}
    for source, offset in HOPS:
        block[source ^ offset] = hop(block[source], offset)

    kept, arrived, hidden, other_hidden, terms = {}, {}, {}, {}, {}
    for step, i in STEPS:
        if step == "hop":
            source, offset = i
            again = core(copy_kernel, of((rows, features)), block[source], cost=0.2)
            block[source ^ offset] = hop(again, offset)
            continue
        if step == "sum":
            total = core(sum_kernel, of((rows, features)), mixed_rows, *terms[0])
            continue
        if step == "got":
            core.also.append(terms[0][i])
            continue
        if step == "pin":
            core.also.append(other_hidden[i])
            continue
        if step == "later":
            again = core(copy_kernel, of((rows, features)), block[0], cost=0.2)
            for offset in LATER:
                block[offset] = hop(again, offset)
            continue
        if step == "need":
            core.also.append(block[i])
            continue
        if step == "on":
            source, offset = i
            block[source ^ offset] = hop(block[source], offset)
            continue
        chunk = CHUNKS[i % len(CHUNKS)]
        count = len(chunk) * rows
        if step in ("send", "keep"):
            product = core(
                first_kernel,
                of((count, 2 * size + LANES)),
                other if step == "send" else mine,
                gain,
                gate_weight,
                up_weight,
                *[block[offset] for offset in chunk],
                cost=COSTS.get((step, i), FIRST_COST),
            )
            if step == "send":
                arrived[i] = lax.ppermute(product, "exp", swap)
            else:
                kept[i] = product
        elif step == "hidden":
            kernel = functools.partial(hidden_kernel, [position[offset] for offset in chunk])
            hidden[i] = core(kernel, of((count, size)), expert, kept[i], arrived[i], packed, cost=HIDDEN_COST)
            other_hidden[i] = lax.ppermute(hidden[i], "exp", swap)
        else:
            shapes = [of((rows, features), jnp.bfloat16 if o else jnp.float32) for o in chunk]
            arrivals = [(at, term) for at, o in enumerate(chunk) for term in terms.pop(o, [])]
            kernel = functools.partial(both_kernel, [at for at, _ in arrivals])
            out = core(
                kernel,
                shapes,
                mine, other, hidden[i], other_hidden[i], down_weight,
                *[term for _, term in arrivals],
                cost=BOTH_COST,
            )
            for offset, term in zip(chunk, out):
                term = hop(term, SENDS[offset]) if offset else term
                terms.setdefault(offset ^ SENDS[offset], []).append(term)
    return total


def solution(mesh):
    placed = (
        P(("rep", "ctx"), "exp"),
        P(("rep", "ctx"), None),
        P(("rep", "ctx"), None),
        P("rep"),
        P(("rep", "ctx"), "exp"),
        P("exp"),
        P(("rep", "ctx"), None),
        P(("rep", "ctx"), None),
        P("ctx", "exp", None),
        P("ctx", "exp", None),
        P("ctx", None, "exp"),
    )
    small = mesh.shape["exp"] == 2 and mesh.shape["ctx"] == 8
    return jax.shard_map(
        local if small else general, mesh=mesh, in_specs=placed, out_specs=P(("rep", "ctx"), "exp"), check_vma=False
    )
```

```python
import functools
import math

import jax
import jax.numpy as jnp
from jax import lax
from jax.experimental import pallas as pl
from jax.experimental.pallas import tpu as pltpu
from jax.sharding import PartitionSpec as P

D = 4096
QUERY_HEADS = 32
KEY_VALUE_HEADS = 2
HEAD_SIZE = 128
TOPK = 8

MASKED_SCORE = -1e30
NORM_EPS = 1e-06
LANES = 128
KERNEL_BYTES = 16 * 1024 * 1024
EXPERT_ROWS = 16
HELD = False
COST = 2e9
FIRST_COST = 1.2
HIDDEN_COST = 0.4
BOTH_COST = 1.1
PACK_COST = 10
ATT_COST = 5
HOPS = ((0, 4), (0, 1), (4, 2), (4, 1), (5, 2), (0, 2), (2, 1))
COSTS = {}
LATER = (2,)
CHUNKS = ((0,), (2, 1), (6, 5), (7,), (4,), (3,))
SENDS = {0: 0, 1: 1, 2: 2, 3: 3, 4: 4, 5: 1, 6: 2, 7: 3}
STEPS = (
    ("send", 0),
    ("keep", 0),
    ("send", 1),
    ("hidden", 0),
    ("keep", 1),
    ("send", 2),
    ("both", 0),
    ("hidden", 1),
    ("keep", 2),
    ("send", 3),
    ("hidden", 2),
    ("both", 1),
    ("keep", 3),
    ("hidden", 3),
    ("send", 4),
    ("both", 2),
    ("both", 3),
    ("got", 1),
    ("got", 2),
    ("keep", 4),
    ("hidden", 4),
    ("send", 5),
    ("both", 4),
    ("keep", 5),
    ("hidden", 5),
    ("both", 5),
    ("sum", 0),
)
def xor_pairs(count, bit):
    return [(i, i ^ bit) for i in range(count)]


def bits_of(count):
    bits = []
    bit = count // 2
    while bit:
        bits.append(bit)
        bit //= 2
    return bits


def gather_rows(block, count):
    for bit in bits_of(count):
        block = jnp.concatenate([block, lax.ppermute(block, "ctx", xor_pairs(count, bit))], axis=0)
    return block


def offsets(count):
    found = [0]
    for bit in bits_of(count):
        found = found + [offset ^ bit for offset in found]
    return found


def scatter_sums(partial, count):
    for bit in reversed(bits_of(count)):
        half = partial.shape[0] // 2
        arrived = lax.ppermute(partial[half:].astype(jnp.bfloat16), "ctx", xor_pairs(count, bit))
        partial = partial[:half] + arrived.astype(jnp.float32)
    return partial


def routed_at_once(mixed_rows, norm_gain, own_route, gate_weight, up_weight, down_weight):
    ctx_count = lax.axis_size("ctx")
    own_experts, _, hidden_size = gate_weight.shape
    mixed_f = mixed_rows.astype(jnp.float32)
    square_sum = lax.psum(jnp.sum(mixed_f * mixed_f, axis=1), "exp")
    normed = (mixed_f * lax.rsqrt(square_sum[:, None] / D + NORM_EPS) * norm_gain[None, :]).astype(
        jnp.bfloat16
    )
    all_normed = gather_rows(normed, ctx_count)
    share = all_normed.shape[0] // lax.axis_size("exp")
    terms = []
    for k in range(own_experts):
        for weight in (gate_weight, up_weight):
            term = jnp.dot(all_normed, weight[k], preferred_element_type=jnp.float32)
            terms.append(term.astype(jnp.bfloat16))
    sums = lax.psum_scatter(
        jnp.concatenate(terms, axis=1), "exp", scatter_dimension=0, tiled=True
    ).astype(jnp.float32)
    my_route = lax.dynamic_slice_in_dim(own_route, lax.axis_index("exp") * share, share, 0)
    pieces = []
    for k in range(own_experts):
        gate_sum = sums[:, 2 * k * hidden_size : (2 * k + 1) * hidden_size]
        up_sum = sums[:, (2 * k + 1) * hidden_size : (2 * k + 2) * hidden_size]
        pieces.append((jax.nn.silu(gate_sum) * up_sum * my_route[:, k : k + 1]).astype(jnp.bfloat16))
    hidden = lax.all_gather(jnp.concatenate(pieces, axis=1), "exp", axis=0, tiled=True)
    down = down_weight.reshape(own_experts * hidden_size, down_weight.shape[2])
    partial = jnp.dot(hidden, down, preferred_element_type=jnp.float32)
    return scatter_sums(partial, ctx_count)


def general(
    queries,
    key_rows,
    value_head_rows,
    block_order,
    residual,
    norm_gain,
    expert_ids,
    route_weight,
    gate_weight,
    up_weight,
    down_weight,
):
    shard_rows = queries.shape[0]
    ctx_count = lax.axis_size("ctx")
    local_head = queries.shape[1] // HEAD_SIZE
    expert_index = lax.axis_index("exp")
    ctx_index = lax.axis_index("ctx")
    own_experts = gate_weight.shape[0]
    expert_count = ctx_count * own_experts

    key_value_head = expert_index * local_head // (QUERY_HEADS // KEY_VALUE_HEADS)
    my_keys = lax.dynamic_slice_in_dim(key_rows, key_value_head * HEAD_SIZE, HEAD_SIZE, 1)
    my_values = lax.dynamic_slice_in_dim(value_head_rows, key_value_head * HEAD_SIZE, HEAD_SIZE, 1)
    experts = jnp.arange(expert_count, dtype=jnp.int32)
    route = jnp.sum(
        jnp.where(expert_ids[:, :, None] == experts[None, None, :], route_weight[:, :, None], 0.0),
        axis=1,
    )
    route_high = lax.reduce_precision(route, 8, 7)
    route_low = route - route_high
    packed = jnp.concatenate(
        [my_keys, my_values, route_high.astype(jnp.bfloat16), route_low.astype(jnp.bfloat16)], axis=1
    )
    gathered = gather_rows(packed, ctx_count)
    all_keys = gathered[:, :HEAD_SIZE]
    all_values = gathered[:, HEAD_SIZE : 2 * HEAD_SIZE]
    all_route = gathered[:, 2 * HEAD_SIZE :].astype(jnp.float32)
    all_route = all_route[:, :expert_count] + all_route[:, expert_count:]
    own_route = lax.dynamic_slice_in_dim(all_route, ctx_index * own_experts, own_experts, 1)

    owners = jnp.array(offsets(ctx_count), jnp.int32) ^ ctx_index
    block_ids = jnp.arange(ctx_count, dtype=jnp.int32)
    key_block = jnp.sum(
        jnp.where(owners[:, None] == block_ids[None, :], block_order[None, :], 0), axis=1
    )
    own_block = key_block[0]
    local_rows = jnp.arange(shard_rows, dtype=jnp.int32)
    query_pos = jnp.tile(own_block * shard_rows + local_rows, local_head)
    key_pos = (key_block[:, None] * shard_rows + local_rows[None, :]).reshape(-1)
    query_flat = (
        queries.reshape(shard_rows, local_head, HEAD_SIZE)
        .transpose(1, 0, 2)
        .reshape(local_head * shard_rows, HEAD_SIZE)
    )
    inv_scale = 1.0 / math.sqrt(HEAD_SIZE)
    visible = key_pos[None, :] <= query_pos[:, None]
    scores = (
        lax.dot_general(
            query_flat, all_keys, (((1,), (1,)), ((), ())), preferred_element_type=jnp.float32
        )
        * inv_scale
    )
    scores = jnp.where(visible, scores, MASKED_SCORE)
    newest = jnp.max(scores, axis=1)
    weights = jnp.where(visible, jnp.exp(scores - newest[:, None]), 0.0)
    weight_sum = jnp.sum(weights, axis=1)
    weighted = jnp.dot(weights.astype(jnp.bfloat16), all_values, preferred_element_type=jnp.float32)
    attention = (
        (weighted / weight_sum[:, None])
        .reshape(local_head, shard_rows, HEAD_SIZE)
        .transpose(1, 0, 2)
        .reshape(shard_rows, local_head * HEAD_SIZE)
        .astype(jnp.bfloat16)
    )
    mixed_rows = (residual.astype(jnp.float32) + attention.astype(jnp.float32)).astype(jnp.bfloat16)
    mixed_f = mixed_rows.astype(jnp.float32)
    routed_sum = routed_at_once(
        mixed_rows, norm_gain, own_route, gate_weight, up_weight, down_weight
    )
    return (mixed_f + routed_sum).astype(jnp.bfloat16)


def pack_kernel(key_ref, value_ref, route_ref, out_ref):
    rows = key_ref.shape[0]
    out_ref[:rows] = key_ref[...]
    out_ref[rows : 2 * rows] = value_ref[...]
    out_ref[2 * rows :] = route_ref[...]


def attention_kernel(place_ref, order_ref, query_ref, packed_ref, residual_ref, out_ref):
    rows = query_ref.shape[0]
    heads = query_ref.shape[1] // HEAD_SIZE
    block = 2 * rows + EXPERT_ROWS
    starts = range(0, packed_ref.shape[0], block)
    count = len(starts) * rows
    keys = jnp.concatenate([packed_ref[i : i + rows] for i in starts], axis=0)
    values = jnp.concatenate([packed_ref[i + rows : i + 2 * rows] for i in starts], axis=0)
    queries = jnp.concatenate(
        [query_ref[:, h * HEAD_SIZE : (h + 1) * HEAD_SIZE] for h in range(heads)], axis=0
    )
    scores = lax.dot_general(
        queries,
        keys,
        (((1,), (1,)), ((), ())),
        preferred_element_type=jnp.float32,
    ) * (1.0 / math.sqrt(HEAD_SIZE))
    me = place_ref[0]
    column = lax.broadcasted_iota(jnp.int32, (rows, count), 1)
    key_pos = column % rows
    for i, offset in enumerate(offsets(count // rows)):
        key_pos = key_pos + jnp.where(column // rows == i, order_ref[me ^ offset] * rows, 0)
    query_pos = order_ref[me] * rows + lax.broadcasted_iota(jnp.int32, (rows, count), 0)
    hidden_score = jnp.where(key_pos <= query_pos, 0.0, MASKED_SCORE)
    scores = scores + jnp.concatenate([hidden_score] * heads, axis=0)
    largest = jnp.max(scores, axis=1, keepdims=True)
    weights = jnp.exp(scores - largest)
    weight_sum = jnp.sum(weights, axis=1, keepdims=True)
    weighted = jnp.dot(
        weights.astype(jnp.bfloat16),
        values,
        preferred_element_type=jnp.float32,
    )
    attention = (weighted / weight_sum).astype(jnp.bfloat16)
    for h in range(heads):
        columns = slice(h * HEAD_SIZE, (h + 1) * HEAD_SIZE)
        part = attention[h * rows : (h + 1) * rows].astype(jnp.float32)
        out_ref[:, columns] = (residual_ref[:, columns].astype(jnp.float32) + part).astype(
            jnp.bfloat16
        )


def copy_kernel(block_ref, out_ref):
    out_ref[...] = block_ref[...]


def product(rows, weight):
    count = rows.shape[0]
    if count < LANES:
        rows = jnp.concatenate([rows, rows], axis=0)
    return jnp.dot(rows, weight, preferred_element_type=jnp.float32)[:count]


def prepared(blocks, gain_ref):
    rows = jnp.concatenate([block[...] for block in blocks], axis=0).astype(jnp.float32)
    squares = jnp.sum(rows * rows, axis=1, keepdims=True)
    return (rows * gain_ref[...]).astype(jnp.bfloat16), squares


def first_kernel(index_ref, gain_ref, gate_ref, up_ref, *rest):
    out_ref = rest[-1]
    k = index_ref[0]
    size = gate_ref.shape[2]
    rows, squares = prepared(rest[:-1], gain_ref)
    gate = product(rows, gate_ref[k])
    out_ref[:, :size] = gate.astype(jnp.bfloat16)
    up = product(rows, up_ref[k])
    out_ref[:, size : 2 * size] = up.astype(jnp.bfloat16)
    high = squares.astype(jnp.bfloat16).astype(jnp.float32)
    lane = lax.broadcasted_iota(jnp.int32, (rows.shape[0], LANES), 1)
    out_ref[:, 2 * size :] = jnp.where(lane == 0, high, squares - high).astype(jnp.bfloat16)


def hidden_kernel(places, index_ref, kept_ref, arrived_ref, packed_ref, out_ref):
    size = out_ref.shape[1]
    rows = out_ref.shape[0] // len(places)
    tail = kept_ref[:, 2 * size :].astype(jnp.float32) + arrived_ref[:, 2 * size :].astype(
        jnp.float32
    )
    scale = lax.rsqrt((tail[:, :1] + tail[:, 1:2]) / D + NORM_EPS)
    block = 2 * rows + EXPERT_ROWS
    expert = lax.broadcasted_iota(jnp.int32, (EXPERT_ROWS, 2 * rows), 0)
    row = lax.broadcasted_iota(jnp.int32, (rows, 2 * rows), 0)
    lane = lax.broadcasted_iota(jnp.int32, (rows, 2 * rows), 1)
    columns = []
    for place in places:
        part = packed_ref[place * block + 2 * rows : (place + 1) * block].astype(jnp.float32)
        line = jnp.sum(jnp.where(expert == index_ref[0], part, 0.0), axis=0, keepdims=True)
        columns.append(jnp.sum(jnp.where(lane % rows == row, line, 0.0), axis=1, keepdims=True))
    route = jnp.concatenate(columns, axis=0)
    gate = kept_ref[:, :size].astype(jnp.float32) + arrived_ref[:, :size].astype(jnp.float32)
    up = kept_ref[:, size : 2 * size].astype(jnp.float32) + arrived_ref[
        :, size : 2 * size
    ].astype(jnp.float32)
    gate = gate * scale
    up = up * (scale * route)
    out_ref[...] = (gate / (1.0 + jnp.exp(-gate)) * up).astype(jnp.bfloat16)


def sum_kernel(mixed_ref, *rest):
    total = mixed_ref[...].astype(jnp.float32)
    for term_ref in rest[:-1]:
        total = total + term_ref[...].astype(jnp.float32)
    rest[-1][...] = total.astype(rest[-1].dtype)


def both_kernel(places, mine_ref, other_ref, hidden_ref, other_hidden_ref, down_ref, *rest):
    both = product(hidden_ref[...], down_ref[mine_ref[0]])
    both = both + product(other_hidden_ref[...], down_ref[other_ref[0]])
    rows = rest[-1].shape[0]
    for i, out_ref in enumerate(rest[len(places) :]):
        term = both[i * rows : (i + 1) * rows]
        for place, term_ref in zip(places, rest):
            if place == i:
                term = term + term_ref[...].astype(jnp.float32)
        out_ref[...] = term.astype(out_ref.dtype)


class Core:
    def __init__(self):
        self.before = None
        self.also = []

    def __call__(self, kernel, out_shape, *args, held=(), cost=0):
        vmem = pl.BlockSpec(memory_space=pltpu.VMEM)
        specs = [
            pl.BlockSpec(memory_space=pltpu.SMEM) if arg.ndim == 1 else vmem for arg in args
        ]
        unread = list(held) + ([] if self.before is None else [self.before]) + self.also
        self.also = []
        specs += [vmem] * len(held) + [pl.BlockSpec(memory_space=pl.ANY)] * (len(unread) - len(held))
        read = len(args)
        many = isinstance(out_shape, list)

        def body(*refs):
            kernel(*refs[:read], *refs[read + len(unread) :])

        out = pl.pallas_call(
            body,
            out_shape=out_shape,
            in_specs=specs,
            out_specs=[vmem] * len(out_shape) if many else vmem,
            compiler_params=pltpu.CompilerParams(vmem_limit_bytes=KERNEL_BYTES),
            cost_estimate=pl.CostEstimate(
                flops=int(cost * COST), bytes_accessed=0, transcendentals=0
            ),
        )(*args, *unread)
        self.before = out[0] if many else out
        return out


def local(
    queries,
    key_rows,
    value_head_rows,
    block_order,
    residual,
    norm_gain,
    expert_ids,
    route_weight,
    gate_weight,
    up_weight,
    down_weight,
):
    rows, features = queries.shape
    ctx_count = lax.axis_size("ctx")
    size = gate_weight.shape[2]
    mine = lax.axis_index("exp").astype(jnp.int32).reshape(1)
    other = 1 - mine
    place = lax.axis_index("ctx").astype(jnp.int32).reshape(1)
    expert = 2 * place + mine
    swap = [(0, 1), (1, 0)]
    gain = norm_gain.reshape(1, features)
    position = {offset: i for i, offset in enumerate(offsets(ctx_count))}
    core = Core()

    def of(shape, dtype=jnp.bfloat16):
        return jax.ShapeDtypeStruct(shape, dtype)

    def hop(block, offset):
        return lax.ppermute(block, "ctx", xor_pairs(ctx_count, offset))

    columns = mine[0] * HEAD_SIZE
    experts = jnp.arange(EXPERT_ROWS, dtype=jnp.int32)
    named = expert_ids.T[:, None, :] == experts[None, :, None]
    route = jnp.sum(jnp.where(named, route_weight.T[:, None, :], 0.0), axis=0)
    high = lax.reduce_precision(route, 8, 7)
    packed = core(
        pack_kernel,
        of((2 * rows + EXPERT_ROWS, HEAD_SIZE)),
        lax.dynamic_slice_in_dim(key_rows, columns, HEAD_SIZE, 1),
        lax.dynamic_slice_in_dim(value_head_rows, columns, HEAD_SIZE, 1),
        jnp.concatenate([high, route - high], axis=1).astype(jnp.bfloat16),
        cost=PACK_COST,
    )
    packed = gather_rows(packed, ctx_count)
    mixed_rows = core(
        attention_kernel,
        of((rows, features)),
        place,
        block_order,
        queries,
        packed,
        residual,
        held=(gate_weight, up_weight) if HELD else (),
        cost=ATT_COST,
    )

    block = {0: mixed_rows}
    for source, offset in HOPS:
        block[source ^ offset] = hop(block[source], offset)

    kept, arrived, hidden, other_hidden, terms = {}, {}, {}, {}, {}
    for step, i in STEPS:
        if step == "hop":
            source, offset = i
            again = core(copy_kernel, of((rows, features)), block[source], cost=0.2)
            block[source ^ offset] = hop(again, offset)
            continue
        if step == "sum":
            total = core(sum_kernel, of((rows, features)), mixed_rows, *terms[0])
            continue
        if step == "got":
            core.also.append(terms[0][i])
            continue
        if step == "pin":
            core.also.append(other_hidden[i])
            continue
        if step == "later":
            again = core(copy_kernel, of((rows, features)), block[0], cost=0.2)
            for offset in LATER:
                block[offset] = hop(again, offset)
            continue
        if step == "need":
            core.also.append(block[i])
            continue
        if step == "on":
            source, offset = i
            block[source ^ offset] = hop(block[source], offset)
            continue
        chunk = CHUNKS[i % len(CHUNKS)]
        count = len(chunk) * rows
        if step in ("send", "keep"):
            product = core(
                first_kernel,
                of((count, 2 * size + LANES)),
                other if step == "send" else mine,
                gain,
                gate_weight,
                up_weight,
                *[block[offset] for offset in chunk],
                cost=COSTS.get((step, i), FIRST_COST),
            )
            if step == "send":
                arrived[i] = lax.ppermute(product, "exp", swap)
            else:
                kept[i] = product
        elif step == "hidden":
            kernel = functools.partial(hidden_kernel, [position[offset] for offset in chunk])
            hidden[i] = core(kernel, of((count, size)), expert, kept[i], arrived[i], packed, cost=HIDDEN_COST)
            other_hidden[i] = lax.ppermute(hidden[i], "exp", swap)
        else:
            shapes = [of((rows, features), jnp.bfloat16 if o else jnp.float32) for o in chunk]
            arrivals = [(at, term) for at, o in enumerate(chunk) for term in terms.pop(o, [])]
            kernel = functools.partial(both_kernel, [at for at, _ in arrivals])
            out = core(
                kernel,
                shapes,
                mine, other, hidden[i], other_hidden[i], down_weight,
                *[term for _, term in arrivals],
                cost=BOTH_COST,
            )
            for offset, term in zip(chunk, out):
                term = hop(term, SENDS[offset]) if offset else term
                terms.setdefault(offset ^ SENDS[offset], []).append(term)
    return total


def solution(mesh):
    placed = (
        P(("rep", "ctx"), "exp"),
        P(("rep", "ctx"), None),
        P(("rep", "ctx"), None),
        P("rep"),
        P(("rep", "ctx"), "exp"),
        P("exp"),
        P(("rep", "ctx"), None),
        P(("rep", "ctx"), None),
        P("ctx", "exp", None),
        P("ctx", "exp", None),
        P("ctx", None, "exp"),
    )
    small = mesh.shape["exp"] == 2 and mesh.shape["ctx"] == 8
    return jax.shard_map(
        local if small else general, mesh=mesh, in_specs=placed, out_specs=P(("rep", "ctx"), "exp"), check_vma=False
    )
```

```python
import functools
import math

import jax
import jax.numpy as jnp
from jax import lax
from jax.experimental import pallas as pl
from jax.experimental.pallas import tpu as pltpu
from jax.sharding import PartitionSpec as P

D = 4096
QUERY_HEADS = 32
KEY_VALUE_HEADS = 2
HEAD_SIZE = 128
TOPK = 8

MASKED_SCORE = -1e30
NORM_EPS = 1e-06
LANES = 128
KERNEL_BYTES = 16 * 1024 * 1024
EXPERT_ROWS = 16
HELD = False
COST = 2e9
FIRST_COST = 1.2
HIDDEN_COST = 0.4
BOTH_COST = 1.1
PACK_COST = 10
ATT_COST = 5
HOPS = ((0, 4), (0, 1), (4, 2), (4, 1), (5, 2), (0, 2), (2, 1))
COSTS = {}
LATER = (2,)
CHUNKS = ((0,), (2, 1), (6, 5), (7,), (4,), (3,))
SENDS = {0: 0, 1: 1, 2: 2, 3: 3, 4: 4, 5: 1, 6: 2, 7: 3}
STEPS = (
    ("send", 0),
    ("keep", 0),
    ("send", 1),
    ("hidden", 0),
    ("keep", 1),
    ("send", 2),
    ("both", 0),
    ("hidden", 1),
    ("keep", 2),
    ("send", 3),
    ("hidden", 2),
    ("keep", 3),
    ("both", 1),
    ("hidden", 3),
    ("send", 4),
    ("both", 2),
    ("both", 3),
    ("got", 1),
    ("got", 2),
    ("keep", 4),
    ("hidden", 4),
    ("send", 5),
    ("keep", 5),
    ("both", 4),
    ("hidden", 5),
    ("both", 5),
    ("sum", 0),
)
def xor_pairs(count, bit):
    return [(i, i ^ bit) for i in range(count)]


def bits_of(count):
    bits = []
    bit = count // 2
    while bit:
        bits.append(bit)
        bit //= 2
    return bits


def gather_rows(block, count):
    for bit in bits_of(count):
        block = jnp.concatenate([block, lax.ppermute(block, "ctx", xor_pairs(count, bit))], axis=0)
    return block


def offsets(count):
    found = [0]
    for bit in bits_of(count):
        found = found + [offset ^ bit for offset in found]
    return found


def scatter_sums(partial, count):
    for bit in reversed(bits_of(count)):
        half = partial.shape[0] // 2
        arrived = lax.ppermute(partial[half:].astype(jnp.bfloat16), "ctx", xor_pairs(count, bit))
        partial = partial[:half] + arrived.astype(jnp.float32)
    return partial


def routed_at_once(mixed_rows, norm_gain, own_route, gate_weight, up_weight, down_weight):
    ctx_count = lax.axis_size("ctx")
    own_experts, _, hidden_size = gate_weight.shape
    mixed_f = mixed_rows.astype(jnp.float32)
    square_sum = lax.psum(jnp.sum(mixed_f * mixed_f, axis=1), "exp")
    normed = (mixed_f * lax.rsqrt(square_sum[:, None] / D + NORM_EPS) * norm_gain[None, :]).astype(
        jnp.bfloat16
    )
    all_normed = gather_rows(normed, ctx_count)
    share = all_normed.shape[0] // lax.axis_size("exp")
    terms = []
    for k in range(own_experts):
        for weight in (gate_weight, up_weight):
            term = jnp.dot(all_normed, weight[k], preferred_element_type=jnp.float32)
            terms.append(term.astype(jnp.bfloat16))
    sums = lax.psum_scatter(
        jnp.concatenate(terms, axis=1), "exp", scatter_dimension=0, tiled=True
    ).astype(jnp.float32)
    my_route = lax.dynamic_slice_in_dim(own_route, lax.axis_index("exp") * share, share, 0)
    pieces = []
    for k in range(own_experts):
        gate_sum = sums[:, 2 * k * hidden_size : (2 * k + 1) * hidden_size]
        up_sum = sums[:, (2 * k + 1) * hidden_size : (2 * k + 2) * hidden_size]
        pieces.append((jax.nn.silu(gate_sum) * up_sum * my_route[:, k : k + 1]).astype(jnp.bfloat16))
    hidden = lax.all_gather(jnp.concatenate(pieces, axis=1), "exp", axis=0, tiled=True)
    down = down_weight.reshape(own_experts * hidden_size, down_weight.shape[2])
    partial = jnp.dot(hidden, down, preferred_element_type=jnp.float32)
    return scatter_sums(partial, ctx_count)


def general(
    queries,
    key_rows,
    value_head_rows,
    block_order,
    residual,
    norm_gain,
    expert_ids,
    route_weight,
    gate_weight,
    up_weight,
    down_weight,
):
    shard_rows = queries.shape[0]
    ctx_count = lax.axis_size("ctx")
    local_head = queries.shape[1] // HEAD_SIZE
    expert_index = lax.axis_index("exp")
    ctx_index = lax.axis_index("ctx")
    own_experts = gate_weight.shape[0]
    expert_count = ctx_count * own_experts

    key_value_head = expert_index * local_head // (QUERY_HEADS // KEY_VALUE_HEADS)
    my_keys = lax.dynamic_slice_in_dim(key_rows, key_value_head * HEAD_SIZE, HEAD_SIZE, 1)
    my_values = lax.dynamic_slice_in_dim(value_head_rows, key_value_head * HEAD_SIZE, HEAD_SIZE, 1)
    experts = jnp.arange(expert_count, dtype=jnp.int32)
    route = jnp.sum(
        jnp.where(expert_ids[:, :, None] == experts[None, None, :], route_weight[:, :, None], 0.0),
        axis=1,
    )
    route_high = lax.reduce_precision(route, 8, 7)
    route_low = route - route_high
    packed = jnp.concatenate(
        [my_keys, my_values, route_high.astype(jnp.bfloat16), route_low.astype(jnp.bfloat16)], axis=1
    )
    gathered = gather_rows(packed, ctx_count)
    all_keys = gathered[:, :HEAD_SIZE]
    all_values = gathered[:, HEAD_SIZE : 2 * HEAD_SIZE]
    all_route = gathered[:, 2 * HEAD_SIZE :].astype(jnp.float32)
    all_route = all_route[:, :expert_count] + all_route[:, expert_count:]
    own_route = lax.dynamic_slice_in_dim(all_route, ctx_index * own_experts, own_experts, 1)

    owners = jnp.array(offsets(ctx_count), jnp.int32) ^ ctx_index
    block_ids = jnp.arange(ctx_count, dtype=jnp.int32)
    key_block = jnp.sum(
        jnp.where(owners[:, None] == block_ids[None, :], block_order[None, :], 0), axis=1
    )
    own_block = key_block[0]
    local_rows = jnp.arange(shard_rows, dtype=jnp.int32)
    query_pos = jnp.tile(own_block * shard_rows + local_rows, local_head)
    key_pos = (key_block[:, None] * shard_rows + local_rows[None, :]).reshape(-1)
    query_flat = (
        queries.reshape(shard_rows, local_head, HEAD_SIZE)
        .transpose(1, 0, 2)
        .reshape(local_head * shard_rows, HEAD_SIZE)
    )
    inv_scale = 1.0 / math.sqrt(HEAD_SIZE)
    visible = key_pos[None, :] <= query_pos[:, None]
    scores = (
        lax.dot_general(
            query_flat, all_keys, (((1,), (1,)), ((), ())), preferred_element_type=jnp.float32
        )
        * inv_scale
    )
    scores = jnp.where(visible, scores, MASKED_SCORE)
    newest = jnp.max(scores, axis=1)
    weights = jnp.where(visible, jnp.exp(scores - newest[:, None]), 0.0)
    weight_sum = jnp.sum(weights, axis=1)
    weighted = jnp.dot(weights.astype(jnp.bfloat16), all_values, preferred_element_type=jnp.float32)
    attention = (
        (weighted / weight_sum[:, None])
        .reshape(local_head, shard_rows, HEAD_SIZE)
        .transpose(1, 0, 2)
        .reshape(shard_rows, local_head * HEAD_SIZE)
        .astype(jnp.bfloat16)
    )
    mixed_rows = (residual.astype(jnp.float32) + attention.astype(jnp.float32)).astype(jnp.bfloat16)
    mixed_f = mixed_rows.astype(jnp.float32)
    routed_sum = routed_at_once(
        mixed_rows, norm_gain, own_route, gate_weight, up_weight, down_weight
    )
    return (mixed_f + routed_sum).astype(jnp.bfloat16)


def pack_kernel(key_ref, value_ref, route_ref, out_ref):
    rows = key_ref.shape[0]
    out_ref[:rows] = key_ref[...]
    out_ref[rows : 2 * rows] = value_ref[...]
    out_ref[2 * rows :] = route_ref[...]


def attention_kernel(place_ref, order_ref, query_ref, packed_ref, residual_ref, out_ref):
    rows = query_ref.shape[0]
    heads = query_ref.shape[1] // HEAD_SIZE
    block = 2 * rows + EXPERT_ROWS
    starts = range(0, packed_ref.shape[0], block)
    count = len(starts) * rows
    keys = jnp.concatenate([packed_ref[i : i + rows] for i in starts], axis=0)
    values = jnp.concatenate([packed_ref[i + rows : i + 2 * rows] for i in starts], axis=0)
    queries = jnp.concatenate(
        [query_ref[:, h * HEAD_SIZE : (h + 1) * HEAD_SIZE] for h in range(heads)], axis=0
    )
    scores = lax.dot_general(
        queries,
        keys,
        (((1,), (1,)), ((), ())),
        preferred_element_type=jnp.float32,
    ) * (1.0 / math.sqrt(HEAD_SIZE))
    me = place_ref[0]
    column = lax.broadcasted_iota(jnp.int32, (rows, count), 1)
    key_pos = column % rows
    for i, offset in enumerate(offsets(count // rows)):
        key_pos = key_pos + jnp.where(column // rows == i, order_ref[me ^ offset] * rows, 0)
    query_pos = order_ref[me] * rows + lax.broadcasted_iota(jnp.int32, (rows, count), 0)
    hidden_score = jnp.where(key_pos <= query_pos, 0.0, MASKED_SCORE)
    scores = scores + jnp.concatenate([hidden_score] * heads, axis=0)
    largest = jnp.max(scores, axis=1, keepdims=True)
    weights = jnp.exp(scores - largest)
    weight_sum = jnp.sum(weights, axis=1, keepdims=True)
    weighted = jnp.dot(
        weights.astype(jnp.bfloat16),
        values,
        preferred_element_type=jnp.float32,
    )
    attention = (weighted / weight_sum).astype(jnp.bfloat16)
    for h in range(heads):
        columns = slice(h * HEAD_SIZE, (h + 1) * HEAD_SIZE)
        part = attention[h * rows : (h + 1) * rows].astype(jnp.float32)
        out_ref[:, columns] = (residual_ref[:, columns].astype(jnp.float32) + part).astype(
            jnp.bfloat16
        )


def copy_kernel(block_ref, out_ref):
    out_ref[...] = block_ref[...]


def product(rows, weight):
    count = rows.shape[0]
    if count < LANES:
        rows = jnp.concatenate([rows, rows], axis=0)
    return jnp.dot(rows, weight, preferred_element_type=jnp.float32)[:count]


def prepared(blocks, gain_ref):
    rows = jnp.concatenate([block[...] for block in blocks], axis=0).astype(jnp.float32)
    squares = jnp.sum(rows * rows, axis=1, keepdims=True)
    return (rows * gain_ref[...]).astype(jnp.bfloat16), squares


def first_kernel(index_ref, gain_ref, gate_ref, up_ref, *rest):
    out_ref = rest[-1]
    k = index_ref[0]
    size = gate_ref.shape[2]
    rows, squares = prepared(rest[:-1], gain_ref)
    gate = product(rows, gate_ref[k])
    out_ref[:, :size] = gate.astype(jnp.bfloat16)
    up = product(rows, up_ref[k])
    out_ref[:, size : 2 * size] = up.astype(jnp.bfloat16)
    high = squares.astype(jnp.bfloat16).astype(jnp.float32)
    lane = lax.broadcasted_iota(jnp.int32, (rows.shape[0], LANES), 1)
    out_ref[:, 2 * size :] = jnp.where(lane == 0, high, squares - high).astype(jnp.bfloat16)


def hidden_kernel(places, index_ref, kept_ref, arrived_ref, packed_ref, out_ref):
    size = out_ref.shape[1]
    rows = out_ref.shape[0] // len(places)
    tail = kept_ref[:, 2 * size :].astype(jnp.float32) + arrived_ref[:, 2 * size :].astype(
        jnp.float32
    )
    scale = lax.rsqrt((tail[:, :1] + tail[:, 1:2]) / D + NORM_EPS)
    block = 2 * rows + EXPERT_ROWS
    expert = lax.broadcasted_iota(jnp.int32, (EXPERT_ROWS, 2 * rows), 0)
    row = lax.broadcasted_iota(jnp.int32, (rows, 2 * rows), 0)
    lane = lax.broadcasted_iota(jnp.int32, (rows, 2 * rows), 1)
    columns = []
    for place in places:
        part = packed_ref[place * block + 2 * rows : (place + 1) * block].astype(jnp.float32)
        line = jnp.sum(jnp.where(expert == index_ref[0], part, 0.0), axis=0, keepdims=True)
        columns.append(jnp.sum(jnp.where(lane % rows == row, line, 0.0), axis=1, keepdims=True))
    route = jnp.concatenate(columns, axis=0)
    gate = kept_ref[:, :size].astype(jnp.float32) + arrived_ref[:, :size].astype(jnp.float32)
    up = kept_ref[:, size : 2 * size].astype(jnp.float32) + arrived_ref[
        :, size : 2 * size
    ].astype(jnp.float32)
    gate = gate * scale
    up = up * (scale * route)
    out_ref[...] = (gate / (1.0 + jnp.exp(-gate)) * up).astype(jnp.bfloat16)


def sum_kernel(mixed_ref, *rest):
    total = mixed_ref[...].astype(jnp.float32)
    for term_ref in rest[:-1]:
        total = total + term_ref[...].astype(jnp.float32)
    rest[-1][...] = total.astype(rest[-1].dtype)


def both_kernel(places, mine_ref, other_ref, hidden_ref, other_hidden_ref, down_ref, *rest):
    both = product(hidden_ref[...], down_ref[mine_ref[0]])
    both = both + product(other_hidden_ref[...], down_ref[other_ref[0]])
    rows = rest[-1].shape[0]
    for i, out_ref in enumerate(rest[len(places) :]):
        term = both[i * rows : (i + 1) * rows]
        for place, term_ref in zip(places, rest):
            if place == i:
                term = term + term_ref[...].astype(jnp.float32)
        out_ref[...] = term.astype(out_ref.dtype)


class Core:
    def __init__(self):
        self.before = None
        self.also = []

    def __call__(self, kernel, out_shape, *args, held=(), cost=0):
        vmem = pl.BlockSpec(memory_space=pltpu.VMEM)
        specs = [
            pl.BlockSpec(memory_space=pltpu.SMEM) if arg.ndim == 1 else vmem for arg in args
        ]
        unread = list(held) + ([] if self.before is None else [self.before]) + self.also
        self.also = []
        specs += [vmem] * len(held) + [pl.BlockSpec(memory_space=pl.ANY)] * (len(unread) - len(held))
        read = len(args)
        many = isinstance(out_shape, list)

        def body(*refs):
            kernel(*refs[:read], *refs[read + len(unread) :])

        out = pl.pallas_call(
            body,
            out_shape=out_shape,
            in_specs=specs,
            out_specs=[vmem] * len(out_shape) if many else vmem,
            compiler_params=pltpu.CompilerParams(vmem_limit_bytes=KERNEL_BYTES),
            cost_estimate=pl.CostEstimate(
                flops=int(cost * COST), bytes_accessed=0, transcendentals=0
            ),
        )(*args, *unread)
        self.before = out[0] if many else out
        return out


def local(
    queries,
    key_rows,
    value_head_rows,
    block_order,
    residual,
    norm_gain,
    expert_ids,
    route_weight,
    gate_weight,
    up_weight,
    down_weight,
):
    rows, features = queries.shape
    ctx_count = lax.axis_size("ctx")
    size = gate_weight.shape[2]
    mine = lax.axis_index("exp").astype(jnp.int32).reshape(1)
    other = 1 - mine
    place = lax.axis_index("ctx").astype(jnp.int32).reshape(1)
    expert = 2 * place + mine
    swap = [(0, 1), (1, 0)]
    gain = norm_gain.reshape(1, features)
    position = {offset: i for i, offset in enumerate(offsets(ctx_count))}
    core = Core()

    def of(shape, dtype=jnp.bfloat16):
        return jax.ShapeDtypeStruct(shape, dtype)

    def hop(block, offset):
        return lax.ppermute(block, "ctx", xor_pairs(ctx_count, offset))

    columns = mine[0] * HEAD_SIZE
    experts = jnp.arange(EXPERT_ROWS, dtype=jnp.int32)
    named = expert_ids.T[:, None, :] == experts[None, :, None]
    route = jnp.sum(jnp.where(named, route_weight.T[:, None, :], 0.0), axis=0)
    high = lax.reduce_precision(route, 8, 7)
    packed = core(
        pack_kernel,
        of((2 * rows + EXPERT_ROWS, HEAD_SIZE)),
        lax.dynamic_slice_in_dim(key_rows, columns, HEAD_SIZE, 1),
        lax.dynamic_slice_in_dim(value_head_rows, columns, HEAD_SIZE, 1),
        jnp.concatenate([high, route - high], axis=1).astype(jnp.bfloat16),
        cost=PACK_COST,
    )
    packed = gather_rows(packed, ctx_count)
    mixed_rows = core(
        attention_kernel,
        of((rows, features)),
        place,
        block_order,
        queries,
        packed,
        residual,
        held=(gate_weight, up_weight) if HELD else (),
        cost=ATT_COST,
    )

    block = {0: mixed_rows}
    for source, offset in HOPS:
        block[source ^ offset] = hop(block[source], offset)

    kept, arrived, hidden, other_hidden, terms = {}, {}, {}, {}, {}
    for step, i in STEPS:
        if step == "hop":
            source, offset = i
            again = core(copy_kernel, of((rows, features)), block[source], cost=0.2)
            block[source ^ offset] = hop(again, offset)
            continue
        if step == "sum":
            total = core(sum_kernel, of((rows, features)), mixed_rows, *terms[0])
            continue
        if step == "got":
            core.also.append(terms[0][i])
            continue
        if step == "pin":
            core.also.append(other_hidden[i])
            continue
        if step == "later":
            again = core(copy_kernel, of((rows, features)), block[0], cost=0.2)
            for offset in LATER:
                block[offset] = hop(again, offset)
            continue
        if step == "need":
            core.also.append(block[i])
            continue
        if step == "on":
            source, offset = i
            block[source ^ offset] = hop(block[source], offset)
            continue
        chunk = CHUNKS[i % len(CHUNKS)]
        count = len(chunk) * rows
        if step in ("send", "keep"):
            product = core(
                first_kernel,
                of((count, 2 * size + LANES)),
                other if step == "send" else mine,
                gain,
                gate_weight,
                up_weight,
                *[block[offset] for offset in chunk],
                cost=COSTS.get((step, i), FIRST_COST),
            )
            if step == "send":
                arrived[i] = lax.ppermute(product, "exp", swap)
            else:
                kept[i] = product
        elif step == "hidden":
            kernel = functools.partial(hidden_kernel, [position[offset] for offset in chunk])
            hidden[i] = core(kernel, of((count, size)), expert, kept[i], arrived[i], packed, cost=HIDDEN_COST)
            other_hidden[i] = lax.ppermute(hidden[i], "exp", swap)
        else:
            shapes = [of((rows, features), jnp.bfloat16 if o else jnp.float32) for o in chunk]
            arrivals = [(at, term) for at, o in enumerate(chunk) for term in terms.pop(o, [])]
            kernel = functools.partial(both_kernel, [at for at, _ in arrivals])
            out = core(
                kernel,
                shapes,
                mine, other, hidden[i], other_hidden[i], down_weight,
                *[term for _, term in arrivals],
                cost=BOTH_COST,
            )
            for offset, term in zip(chunk, out):
                term = hop(term, SENDS[offset]) if offset else term
                terms.setdefault(offset ^ SENDS[offset], []).append(term)
    return total


def solution(mesh):
    placed = (
        P(("rep", "ctx"), "exp"),
        P(("rep", "ctx"), None),
        P(("rep", "ctx"), None),
        P("rep"),
        P(("rep", "ctx"), "exp"),
        P("exp"),
        P(("rep", "ctx"), None),
        P(("rep", "ctx"), None),
        P("ctx", "exp", None),
        P("ctx", "exp", None),
        P("ctx", None, "exp"),
    )
    small = mesh.shape["exp"] == 2 and mesh.shape["ctx"] == 8
    return jax.shard_map(
        local if small else general, mesh=mesh, in_specs=placed, out_specs=P(("rep", "ctx"), "exp"), check_vma=False
    )
```
